256 devices in a mesh: tm: 32 (over y, x, core), panel: 8 (over z).
Axes of the slice: x: 4, y: 4, z: 8, core: 2. Of those that a mesh axis runs over, the one named last changes fastest.
Arguments:
- inv_diag: bfloat16 [32, 4096, 4096], P('tm', None, 'panel')
- couple: bfloat16 [32, 3, 4, 128, 128], P('tm'), may hold values from -0.25 to 0.25
- col_blocks: int32 [32, 3], replicated, may hold values from 0 to 31, as said below
- row_blocks: int32 [32, 4], P('tm'), may hold values from 0 to 31, as said below
Outputs:
- variances: float32 [32, 4096], P('tm', 'panel')
- schur: float32 [32, 384, 384], P('tm')
The draws below stay inside these ranges and needn't reach their ends.
Inputs may be any that keep to these rules, and one draw needn't show every extreme that they name: Each row holds 4 different block numbers; row_blocks[0] holds 0 and 31. `col_blocks`: each row holds 3 different block numbers; for t >= 1 they are all among row_blocks[t - 1].
All inputs are finite; a program needn't handle non-finite values.
Results may differ from the reference program's by a relative error of at most 0.0003.
Values sent between devices are 32-bit elements; how exact they have to be, the bound alone decides.
A program may use at most 128 MiB of HBM per device.

```python
import jax
import jax.numpy as jnp
from jax import lax

NODES = 4096
BLK = 128
SBLK = 3
KB = 4
STEPS = 32
NBLK = 32
WIDTH = 384


def block_pattern(key):
    key_list = jax.random.split(jax.random.fold_in(key, 11), STEPS + 1)
    permuted = jax.vmap(lambda one: jax.random.permutation(one, NBLK))(key_list)
    rows_all = permuted[:, :KB].astype(jnp.int32)
    inner = jax.random.permutation(jax.random.fold_in(key, 13), NBLK - 2)[:KB - 2].astype(jnp.int32) + 1
    first_rows = jnp.concatenate([jnp.array([0, NBLK - 1], jnp.int32), inner])
    rows_all = rows_all.at[1].set(first_rows)
    order_list = jax.random.split(jax.random.fold_in(key, 12), STEPS)
    orders = jax.vmap(lambda one: jax.random.permutation(one, KB))(order_list).astype(jnp.int32)
    orders = orders.at[1].set(jnp.arange(KB, dtype=jnp.int32))
    chosen = jnp.take_along_axis(rows_all[:STEPS], orders[:, :SBLK], axis=1)
    return (rows_all[1:], chosen)


def draw_row_blocks(key, part):
    return block_pattern(key)[0].astype(jnp.int32)


def draw_col_blocks(key, part):
    return block_pattern(key)[1].astype(jnp.int32)


def draw_inv_diag(key, part):
    key = jax.random.fold_in(key, 5)
    key_diag, key_off = jax.random.split(key, 2)
    row_ids = lax.broadcasted_iota(jnp.int32, (NODES, NODES), 0)
    col_ids = lax.broadcasted_iota(jnp.int32, (NODES, NODES), 1)
    lower = (row_ids > col_ids).astype(jnp.float32)
    on_diag = (row_ids == col_ids).astype(jnp.float32)
    diag_vals = jax.random.uniform(key_diag, (STEPS, 1, NODES), jnp.float32, 0.8, 1.2)
    off_vals = jax.random.normal(key_off, (STEPS, NODES, NODES), jnp.float32)
    whole = on_diag * diag_vals + lower * off_vals * (0.5 / NODES ** 0.5)
    return whole.astype(jnp.bfloat16)


def level_of(own_key, extent, cuts, least, high):
    def one(dim, parts):
        steps = jax.random.uniform(jax.random.fold_in(jax.random.fold_in(own_key, 6), dim), (parts,), jnp.float32, least / len(cuts), high / len(cuts))
        return jnp.repeat(jnp.exp(steps), extent[dim] // parts).reshape((-1,) + (1,) * (len(extent) - dim - 1))

    loudness = one(*cuts[0])
    for cut in cuts[1:]:
        loudness = loudness * one(*cut)
    return loudness


def normal_values(key, dims, scale, limit, cuts=(), held_as=jnp.bfloat16):
    entries = jax.random.normal(key, dims, jnp.float32) * scale
    if len(cuts) > 0:
        entries = level_of(key, dims, cuts, -0.22, 0.18) * entries
    return jnp.clip(entries, min=-limit, max=limit).astype(held_as)


def setup_inputs(seed: int = 0) -> dict:
    seeds = jax.random.split(jax.random.key(seed), 5)
    return {
        "inv_diag": draw_inv_diag(jax.random.fold_in(seeds[4], 71), 0),
        "couple": normal_values(seeds[1], (STEPS, SBLK, KB, BLK, BLK), (WIDTH * 20 // 17) ** -0.5, 0.25, ((0, 32),)),
        "col_blocks": draw_col_blocks(jax.random.fold_in(seeds[4], 71), 0),
        "row_blocks": draw_row_blocks(jax.random.fold_in(seeds[4], 71), 0),
    }


def matmul(left, right):
    return jnp.dot(left, right, precision=lax.Precision.HIGHEST, preferred_element_type=jnp.float32)


def reference(inv_diag, couple, col_blocks, row_blocks):
    nblocks = NODES // BLK
    width = SBLK * BLK
    upcoming_all = jnp.concatenate([col_blocks[1:], col_blocks[-1:]], axis=0)

    def one_step(state, inputs):
        operand, pieces, rows, upcoming = inputs
        hits = (rows[:, None] == jnp.arange(nblocks, dtype=jnp.int32)[None, :]).astype(jnp.float32)
        spread = jnp.einsum("kb,ckij->bicj", hits, pieces.astype(jnp.float32))
        spread = spread.astype(jnp.bfloat16).reshape(NODES, width)
        basis = jnp.dot(operand, spread, preferred_element_type=jnp.float32)
        gram = matmul(basis.T, basis)
        link = jnp.take(basis.reshape(nblocks, BLK, width), upcoming, axis=0).reshape(width, width)
        picked = jnp.take(operand.reshape(nblocks, BLK, NODES), upcoming, axis=0).reshape(width, NODES).astype(jnp.float32)
        column_sq = jnp.sum(jnp.square(operand.astype(jnp.float32)), axis=0)
        variance = column_sq + jnp.sum(picked * matmul(state, picked), axis=0)
        new_state = gram + matmul(link.T, matmul(state, link))
        return new_state, (variance, new_state)

    start = jnp.zeros((width, width), jnp.float32)
    final, outputs = lax.scan(one_step, start, (inv_diag, couple, row_blocks, upcoming_all), reverse=True)
    return outputs[0], outputs[1]
```

```python
import functools

import jax
import jax.numpy as jnp
from jax import lax
from jax.experimental import pallas as pl
from jax.experimental.pallas import tpu as pltpu
from jax.sharding import PartitionSpec as P

MESH = pl.DeviceIdType.MESH
F32 = jnp.float32
BF16 = jnp.bfloat16

ROUTES = (
    (
        (15, 0, 0, -1, 3), (19, 0, 0, -1, 6), (26, 0, 0, 1, 20), (0, 0, 0, 0, 0), (4, 0, 0, 1, 8), (1, 0, 0, 0, 0),
        (2, 0, 0, 0, 0), (3, 0, 0, 0, 0), (22, 0, 0, -1, 9), (6, 0, 0, 1, 11), (30, 0, 0, -1, 11), (7, 0, 0, 1, 14),
        (23, 0, 0, -1, 14), (17, 0, 0, 1, 19), (5, 0, 1, 0, 0), (13, 0, 0, -1, 16), (18, 0, 0, 1, 22), (8, 0, 1, 0, 0),
        (29, 0, 0, -1, 20), (20, 0, 0, 1, 25), (9, 0, 1, 0, 0), (16, 0, 1, -1, 22), (25, 1, 0, 1, 24), (10, 0, 1, 0, 0),
        (12, 0, 0, -1, 27), (27, 0, 0, 1, 26), (11, 0, 1, 0, 0), (21, 0, 1, -1, 28), (28, 1, 0, 1, 29), (14, 1, 1, 0, 0),
        (24, 1, 1, 0, 0), (31, 1, 1, 0, 0),
    ),
    (
        (12, 0, 0, 1, 6), (13, 0, 0, 1, 10), (16, 0, 0, -1, 21), (21, 0, 0, -1, 27), (29, 0, 0, 1, 13), (5, 0, 0, -1, 14),
        (23, 0, 0, 1, 16), (8, 0, 1, -1, 17), (4, 1, 0, 0, 0), (22, 0, 0, 1, 18), (9, 0, 1, -1, 20), (6, 1, 0, 0, 0),
        (30, 0, 0, 1, 21), (10, 0, 1, -1, 23), (7, 1, 0, 0, 0), (15, 0, 0, 1, 23), (11, 0, 1, -1, 26), (19, 0, 0, 1, 26),
        (14, 0, 0, -1, 29), (17, 1, 1, 0, 0), (26, 1, 0, 1, 24), (24, 0, 1, -1, 30), (18, 1, 1, 0, 0), (31, 0, 0, -1, 31),
        (25, 1, 0, 1, 27), (20, 1, 1, 0, 0), (27, 1, 1, 0, 0), None, None, (28, 1, 1, 0, 0),
        None, None,
    ),
    (
        (14, 0, 0, 1, 3), (31, 0, 0, 1, 6), (8, 0, 0, -1, 7), (9, 0, 0, -1, 10), (21, 0, 0, 1, 9), (10, 0, 0, -1, 13),
        (12, 1, 0, 1, 11), (11, 0, 0, -1, 16), (16, 0, 0, 1, 14), (24, 0, 0, -1, 21), (13, 1, 0, 1, 16), (17, 0, 1, -1, 19),
        None, (29, 1, 0, 1, 19), (18, 0, 1, -1, 22), None, (23, 1, 0, 1, 22), (20, 0, 1, -1, 25),
        (22, 1, 0, 1, 25), (27, 0, 1, -1, 26), None, (30, 1, 0, 1, 27), (28, 0, 1, -1, 29), (15, 1, 1, 0, 0),
        (26, 1, 1, 0, 0), None, (19, 1, 1, 0, 0), (25, 1, 1, 0, 0), None, None,
        None, None,
    ),
    (
        (24, 0, 0, 1, 3), (25, 0, 0, -1, 27), None, (14, 1, 0, 1, 7), (17, 0, 1, -1, 11), None,
        (31, 1, 0, 1, 10), (18, 0, 1, -1, 14), None, (21, 1, 0, 1, 12), (20, 0, 1, -1, 17), (12, 1, 0, 1, 15),
        (28, 0, 1, -1, 22), None, (16, 1, 0, 1, 18), (27, 0, 1, -1, 19), (13, 1, 0, 1, 20), (26, 0, 1, -1, 24),
        None, (29, 1, 0, 1, 23), (15, 0, 1, -1, 23), None, (23, 1, 0, 1, 26), (19, 0, 1, -1, 26),
        None, (22, 1, 1, 0, 0), None, (30, 1, 1, 0, 0), None, None,
        None, None,
    ),
    (
        (25, 0, 0, 1, 3), (17, 0, 0, -1, 4), (18, 0, 0, -1, 7), (24, 1, 0, 1, 7), (20, 0, 1, -1, 10), None,
        (28, 0, 1, -1, 12), (14, 1, 0, 1, 11), None, (27, 0, 1, -1, 15), (31, 1, 0, 1, 15), (26, 0, 1, -1, 17),
        (21, 1, 0, 1, 16), None, None, (12, 1, 0, 1, 19), (15, 0, 1, -1, 20), None,
        (16, 1, 0, 1, 21), (19, 0, 1, -1, 23), (13, 1, 0, 1, 24), (22, 0, 1, -1, 25), None, (29, 1, 0, 1, 27),
        (30, 0, 1, -1, 27), None, (23, 1, 1, 0, 0), None, None, None,
        None, None,
    ),
    (
        (20, 0, 0, -1, 4), (28, 0, 0, -1, 6), None, (25, 1, 0, 1, 8), (27, 0, 1, -1, 9), None,
        (26, 0, 1, -1, 11), (24, 1, 0, 1, 11), None, None, None, (14, 1, 0, 1, 15),
        (15, 0, 1, -1, 16), None, (19, 0, 1, -1, 19), (31, 1, 0, 1, 19), (21, 1, 0, 1, 21), (22, 0, 1, -1, 21),
        None, (12, 1, 0, 1, 23), (30, 0, 1, -1, 24), (16, 1, 0, 1, 26), (23, 0, 1, -1, 26), None,
        (13, 1, 1, 0, 0), None, None, (29, 1, 1, 0, 0), None, None,
        None, None,
    ),
    (
        (27, 0, 0, -1, 4), (26, 0, 0, -1, 6), (28, 0, 0, 1, 4), None, None, None,
        None, (15, 0, 1, -1, 12), (25, 1, 0, 1, 12), None, (19, 0, 1, -1, 14), (24, 1, 0, 1, 15),
        (22, 0, 1, -1, 17), None, None, (14, 1, 0, 1, 19), (30, 0, 1, -1, 20), None,
        (23, 0, 1, -1, 22), (31, 1, 0, 1, 23), (13, 0, 1, -1, 24), (21, 1, 0, 1, 28), None, (12, 1, 0, 1, 27),
        (29, 0, 1, -1, 27), None, (16, 1, 1, 0, 0), None, None, None,
        None, None,
    ),
    (
        None, None, None, (15, 0, 1, -1, 7), (28, 1, 0, 1, 28), None,
        (19, 0, 1, -1, 10), None, None, (22, 0, 1, -1, 12), None, (30, 0, 1, -1, 16),
        (25, 1, 0, 1, 22), None, (23, 0, 1, -1, 18), (24, 1, 0, 1, 30), (13, 0, 1, -1, 20), None,
        None, (14, 1, 0, 1, 29), (29, 0, 1, -1, 24), None, (16, 0, 1, -1, 26), (31, 1, 0, 1, 31),
        None, None, None, (12, 1, 1, 0, 0), (21, 1, 1, 0, 0), None,
        None, None,
    ),
)
PAIRS = ((0, 0), (0, 1), (0, 2), (1, 1), (1, 2), (2, 2))


def pick(me, values):
    values = [int(v) for v in values]
    if len(set(values)) == 1:
        return values[0]
    out = jnp.int32(values[-1])
    for p in range(len(values) - 1):
        out = jnp.where(me == p, jnp.int32(values[p]), out)
    return out


def when(cond):
    if isinstance(cond, (bool, int)):
        return (lambda f: f()) if cond else (lambda f: None)
    return pl.when(cond)


def dot(a, b):
    return jnp.dot(a, b, preferred_element_type=F32)


def split(x):
    high = x.astype(BF16)
    return high, (x - high.astype(F32)).astype(BF16)


def kernel(ring, total_steps, inv, couple, cols, rows, var_out, schur_out, spread, picks, squares,
           out, got, link_part, link_full, link_put, link_got, keep_h, keep_l, keep_ht, keep_lt,
           b_put, b_got, a_now, a_put, a_got, mat_h, mat_l, tmp_h, tmp_l, last_put, last_got, last_full,
           state, state_full, send_sem, got_sem, lr_send, lr_recv, lg_send, lg_recv, fr_send, fr_recv,
           fg_send, fg_recv, st_send, st_recv, b_send, b_recv, br_send, a_send, a_recv, ar_send):
    me = lax.axis_index("panel")
    t = lax.axis_index("tm")
    m = t // 2
    core = lax.rem(t, 2)
    chips = total_steps // 2
    blk = couple.shape[2]
    local = inv.shape[2]
    width = 3 * blk
    nlocal = local // blk
    levels = len([d for d in (1, 2, 4, 8, 16) if d < chips])
    right = lax.rem(me + 1, ring)
    left = lax.rem(me + ring - 1, ring)
    mate = t + 1 - 2 * core

    def remote(src, dst, ssem, rsem, **where):
        return pltpu.make_async_remote_copy(src_ref=src, dst_ref=dst, send_sem=ssem, recv_sem=rsem,
                                            device_id=where, device_id_type=MESH)

    def arrived(dst, rsem):
        remote(dst, dst, rsem, rsem, tm=t, panel=me).wait_recv()

    def left_here(src, ssem):
        remote(src, src, ssem, ssem, tm=t, panel=me).wait_send()

    def mod(x):
        return lax.rem(x + 4 * ring, ring)

    barrier = pltpu.get_barrier_semaphore()
    greet = [(True, t, left), (True, t, right), (True, mate, me)]
    greet.append((jnp.logical_and(core == 1, t + 1 < total_steps), t + 1, me))
    greet.append((jnp.logical_and(core == 0, t > 0), t - 1, me))
    for k in range(levels):
        d = 2 ** k
        greet.append((jnp.logical_and(core == 0, m + d < chips), t + 2 * d, me))
        greet.append((jnp.logical_and(core == 0, m >= d), t - 2 * d, me))
    for cond, tt, pp in greet:
        @when(cond)
        def _(tt=tt, pp=pp):
            pl.semaphore_signal(barrier, inc=1, device_id=dict(tm=tt, panel=pp), device_id_type=MESH)

    for b in range(nlocal):
        for c in range(3):
            piece = jnp.zeros((blk, blk), F32)
            for k in range(4):
                off = rows[0, k] - (me * nlocal + b)
                piece = piece + couple[c, k].astype(F32) * (1 - jnp.minimum(off * off, 1)).astype(F32)
            spread[pl.ds(b * blk, blk), pl.ds(c * blk, blk)] = piece.astype(BF16)
    later = jnp.minimum(t + 1, total_steps - 1)
    for c in range(3):
        picks[pl.ds(c * blk, blk), :] = inv[cols[later, c]]
    for c in range(3):
        link_part[pl.ds(c * blk, blk), :] = dot(picks[pl.ds(c * blk, blk), :], spread[...])
    a_now[...] = jnp.zeros_like(a_now)

    peers = jnp.int32(0)
    for cond, tt, pp in greet:
        peers = peers + (1 if cond is True else cond.astype(jnp.int32))
    pl.semaphore_wait(barrier, peers)

    def reduce_step(s, part, size, put, recv, ssem, rsem):
        for way in range(2):
            if s >= 4 - way:
                continue
            nbr = right if way == 0 else left
            r = mod(me + 4 - s) if way == 0 else mod(me - 3 + s)
            src = part.at[pl.ds(pl.multiple_of(r * size, 8), size), :]
            j = 4 * way + s
            if s > 0:
                arrived(recv.at[j - 1], rsem.at[j - 1])
                put[j] = src[...] + recv[j - 1]
                src = put.at[j]
            remote(src, recv.at[j], ssem.at[j], rsem.at[j], panel=nbr).start()

    def reduce_end(part, size, recv, rsem, dest):
        arrived(recv.at[3], rsem.at[3])
        arrived(recv.at[6], rsem.at[6])
        at = pl.ds(pl.multiple_of(me * size, 8), size)
        dest[at, :] = part[at, :] + recv[3] + recv[6]

    def gather_step(s, dest, size, ssem, rsem, done):
        for way in range(2):
            if s >= 4 - way:
                continue
            nbr = right if way == 0 else left
            r = mod(me - s) if way == 0 else mod(me + s)
            at = pl.ds(pl.multiple_of(r * size, 8), size)
            j = 4 * way + s
            if s > 0:
                arrived(dest.at[at, :], rsem.at[j - 1])
            remote(dest.at[at, :], dest.at[at, :], ssem.at[j], rsem.at[j], panel=nbr).start()
            if done is not None and (s > 0 or way == 0):
                done(j, at)

    def gather_end(dest, size, rsem, done):
        for way in range(2):
            j = 3 + 3 * way
            r = mod(me - 4) if way == 0 else mod(me + 3)
            at = pl.ds(pl.multiple_of(r * size, 8), size)
            arrived(dest.at[at, :], rsem.at[j])
            if done is not None:
                done(4 + way * 3, at)

    def keep(v, x):
        h, l = split(x)
        keep_h[v] = h
        keep_l[v] = l
        xt = x.T
        h, l = split(xt)
        keep_ht[v] = h
        keep_lt[v] = l

    def times_kept(x, v):
        h, l = split(x)
        return dot(h, keep_h[v]) + dot(h, keep_l[v]) + dot(l, keep_h[v])

    def unpack(src, write):
        for n, (i, j) in enumerate(PAIRS):
            x = src[pl.ds(n * blk, blk), :]
            write(i, j, x)
            if i != j:
                write(j, i, x.T)

    def sandwich(src, v):
        def write(i, j, x):
            h, l = split(x)
            mat_h[pl.ds(i * blk, blk), pl.ds(j * blk, blk)] = h
            mat_l[pl.ds(i * blk, blk), pl.ds(j * blk, blk)] = l
        unpack(src, write)
        x = dot(mat_h[...], keep_h[v]) + dot(mat_h[...], keep_l[v]) + dot(mat_l[...], keep_h[v])
        h, l = split(x)
        tmp_h[...] = h
        tmp_l[...] = l
        n = 0
        for i in range(3):
            rows_i = pl.ds(i * blk, blk)
            cols_i = pl.ds(i * blk, width - i * blk)
            x = (dot(keep_ht[v, rows_i, :], tmp_h[:, cols_i]) + dot(keep_ht[v, rows_i, :], tmp_l[:, cols_i])
                 + dot(keep_lt[v, rows_i, :], tmp_h[:, cols_i]))
            for j in range(3 - i):
                at = pl.ds(n * blk, blk)
                a_now[at, :] = a_now[at, :] + x[:, j * blk:(j + 1) * blk]
                n += 1

    def add_squares(first, count):
        def one(n, total):
            x = inv[n].astype(F32)
            return total + jnp.sum((x * x).reshape(blk // 8, 8, local), axis=0)
        squares[...] = lax.fori_loop(first, first + count, one, squares[...])

    def basis_step(i):
        acts = [ROUTES[p][i] for p in range(ring)]
        active = pick(me, [a is not None for a in acts])
        acts = [a if a is not None else (0, 0, 0, 0, 0) for a in acts]
        steps = got.shape[0] // 2
        goes = pick(me, [a[3] != 0 for a in acts])
        is_root = pick(me, [a[3] == 0 for a in acts])

        @when(active == 1)
        def _():
            row = pick(me, [a[0] for a in acts])
            x = inv[row]
            out[i] = dot(x, spread[...])
            for side in range(2):
                @when(pick(me, [a[1 + side] for a in acts]) == 1)
                def _(side=side):
                    arrived(got.at[side * steps + i], got_sem.at[side * steps + i])
                    out[i] = out[i] + got[side * steps + i]

            @when(goes == 1)
            def _():
                slot = pick(me, [a[4] + (steps if a[3] < 0 else 0) for a in acts])
                to = pick(me, [(p + acts[p][3]) % ring for p in range(ring)])
                remote(out.at[i], got.at[slot], send_sem.at[i], got_sem.at[slot], panel=to).start()

            @when(is_root == 1)
            def _():
                x = out[i]
                h, l = split(x)
                th, tl = split(x.T)
                n = 0
                for b in range(3):
                    y = (dot(th[b * blk:(b + 1) * blk], h[:, b * blk:]) + dot(th[b * blk:(b + 1) * blk], l[:, b * blk:])
                         + dot(tl[b * blk:(b + 1) * blk], h[:, b * blk:]))
                    for j in range(3 - b):
                        at = pl.ds(n * blk, blk)
                        a_now[at, :] = a_now[at, :] + y[:, j * blk:(j + 1) * blk]
                        n += 1

    def b_first():
        @when(core == 1)
        def _():
            remote(link_full, b_got.at[0], b_send.at[0], b_recv.at[0], tm=mate).start()
        keep(0, link_full[...])

    def b_pair():
        @when(core == 0)
        def _():
            arrived(b_got.at[0], b_recv.at[0])
            x = times_kept(b_got[0], 0)
            keep(1, x)
            b_put[0] = x
        @when(core == 1)
        def _():
            keep_h[1] = keep_h[0]
            keep_l[1] = keep_l[0]
            keep_ht[1] = keep_ht[0]
            keep_lt[1] = keep_lt[0]

    def b_sends(k):
        d = 2 ** k
        return jnp.logical_and(core == 0, jnp.logical_and(m >= d, m + d < chips))

    def b_start(k):
        @when(b_sends(k))
        def _():
            remote(b_put.at[k], b_got.at[k + 1], b_send.at[k + 1], b_recv.at[k + 1], tm=t - 2 ** (k + 1)).start()

    def b_relays(k):
        return jnp.logical_and(core == 0, m + 2 ** (k + 1) < chips)

    def b_end(k):
        @when(m + 2 ** (k + 1) < chips)
        def _():
            arrived(b_got.at[k + 1], b_recv.at[k + 1])
            @when(core == 0)
            def _():
                remote(b_got.at[k + 1], b_got.at[k + 1], br_send.at[k], b_recv.at[k + 1], tm=mate).start()
            x = times_kept(b_got[k + 1], k + 1)
            keep(k + 2, x)
            if k + 2 < levels:
                b_put[k + 1] = x

    squares[...] = jnp.zeros_like(squares)
    nsteps = got.shape[0] // 2
    size = width // ring
    nblocks = inv.shape[0]
    extra = {}

    def add(i, f):
        extra.setdefault(i, []).append(f)

    for s in range(4):
        add(1 + s, functools.partial(reduce_step, s, link_part, size, link_put, link_got, lr_send, lr_recv))
    add(5, functools.partial(reduce_end, link_part, size, link_got, lr_recv, link_full))
    for s in range(4):
        add(5 + s, functools.partial(gather_step, s, link_full, size, lg_send, lg_recv, None))
    add(9, functools.partial(gather_end, link_full, size, lg_recv, None))
    add(9, b_first)
    add(10, b_pair)
    for k in range(levels - 1):
        add(10 + 4 * k, functools.partial(b_start, k))
        add(14 + 4 * k, functools.partial(b_end, k))
    for s in range(4):
        add(1 + s, functools.partial(add_squares, s * nblocks // 4, nblocks // 4))
    for i in range(max(nsteps, max(extra))+ 1):
        for f in extra.get(i, []):
            f()
        if i < nsteps:
            basis_step(i)

    @when(core == 1)
    def _():
        a_put[0] = a_now[...]
        remote(a_put.at[0], a_got.at[0], a_send.at[0], a_recv.at[0], tm=mate).start()

    @when(core == 0)
    def _():
        arrived(a_got.at[0], a_recv.at[0])
        sandwich(a_got.at[0], 0)

    for k in range(levels):
        d = 2 ** k
        @when(jnp.logical_and(core == 0, m >= d))
        def _(k=k, d=d):
            a_put[k + 1] = a_now[...]
            remote(a_put.at[k + 1], a_got.at[k + 1], a_send.at[k + 1], a_recv.at[k + 1], tm=t - 2 * d).start()

        @when(m + d < chips)
        def _(k=k):
            arrived(a_got.at[k + 1], a_recv.at[k + 1])
            @when(core == 0)
            def _():
                remote(a_got.at[k + 1], a_got.at[k + 1], ar_send.at[k], a_recv.at[k + 1], tm=mate).start()
            sandwich(a_got.at[k + 1], k + 1)

    size2 = 6 * blk // ring

    def forward(j, at):
        @when(t > 0)
        def _():
            remote(last_full.at[at, :], state.at[at, :], st_send.at[j], st_recv.at[j], tm=t - 1).start()

    for s in range(4):
        reduce_step(s, a_now, size2, last_put, last_got, fr_send, fr_recv)
    reduce_end(a_now, size2, last_got, fr_recv, last_full)
    for s in range(4):
        gather_step(s, last_full, size2, fg_send, fg_recv, forward)
    gather_end(last_full, size2, fg_recv, forward)

    def write_schur(i, j, x):
        schur_out[pl.ds(i * blk, blk), pl.ds(j * blk, blk)] = x
    unpack(last_full, write_schur)

    pieces = [mod(me - s) for s in range(4)] + [mod(me - 4)] + [mod(me + s) for s in range(1, 3)] + [mod(me + 3)]
    slots = [0, 1, 2, 3, 4, 5, 6, 7]

    @when(t + 1 < total_steps)
    def _():
        for j, r in zip(slots, pieces):
            at = pl.ds(pl.multiple_of(r * size2, 8), size2)
            arrived(state.at[at, :], st_recv.at[j])

    @when(t + 1 == total_steps)
    def _():
        state[...] = jnp.zeros_like(state)

    def write_state(i, j, x):
        h, l = split(x)
        mat_h[pl.ds(i * blk, blk), pl.ds(j * blk, blk)] = h
        mat_l[pl.ds(i * blk, blk), pl.ds(j * blk, blk)] = l
    unpack(state, write_state)
    total = jnp.sum(squares[...], axis=0, keepdims=True)
    y = dot(mat_h[...], picks[...]) + dot(mat_l[...], picks[...])
    var_out[...] = total + jnp.sum(picks[...].astype(F32) * y, axis=0, keepdims=True)

    for i in range(nsteps):
        acts = [ROUTES[p][i] or (0, 0, 0, 0, 0) for p in range(ring)]
        @when(pick(me, [a[3] != 0 for a in acts]) == 1)
        def _(i=i):
            left_here(out.at[i], send_sem.at[i])
    for j in range(7):
        left_here(link_got.at[j], lr_send.at[j])
        left_here(link_got.at[j], lg_send.at[j])
        left_here(last_got.at[j], fr_send.at[j])
        left_here(last_got.at[j], fg_send.at[j])

    @when(t > 0)
    def _():
        for j in range(8):
            left_here(last_got.at[0], st_send.at[j])

    @when(core == 1)
    def _():
        left_here(b_got.at[0], b_send.at[0])
        left_here(a_got.at[0], a_send.at[0])
    for k in range(levels):
        d = 2 ** k
        if k < levels - 1:
            @when(b_sends(k))
            def _(k=k):
                left_here(b_got.at[k + 1], b_send.at[k + 1])
            @when(b_relays(k))
            def _(k=k):
                left_here(b_got.at[k + 1], br_send.at[k])
        @when(jnp.logical_and(core == 0, m >= d))
        def _(k=k):
            left_here(a_got.at[k + 1], a_send.at[k + 1])
        @when(jnp.logical_and(core == 0, m + d < chips))
        def _(k=k):
            left_here(a_got.at[k + 1], ar_send.at[k])


def per_device(ring, inv_diag, couple, col_blocks, row_blocks):
    nodes, local = inv_diag.shape[1], inv_diag.shape[2]
    blk = couple.shape[3]
    width = couple.shape[1] * blk
    total_steps = col_blocks.shape[0]
    chips = total_steps // 2
    levels = len([d for d in (1, 2, 4, 8, 16) if d < chips])
    nsteps = max(len(r) for r in ROUTES)
    piece, piece2 = width // ring, 6 * blk // ring
    vm, dma = pltpu.VMEM, pltpu.SemaphoreType.DMA
    packed = (6 * blk, blk)
    scratch = [
        vm((local, width), BF16), vm((width, local), BF16), vm((8, local), F32),
        vm((nsteps, blk, width), F32), vm((2 * nsteps, blk, width), F32),
        vm((width, width), F32), vm((width, width), F32), vm((7, piece, width), F32), vm((7, piece, width), F32),
        vm((levels + 1, width, width), BF16), vm((levels + 1, width, width), BF16),
        vm((levels + 1, width, width), BF16), vm((levels + 1, width, width), BF16),
        vm((levels, width, width), F32), vm((levels, width, width), F32),
        vm(packed, F32), vm((levels + 1,) + packed, F32), vm((levels + 1,) + packed, F32),
        vm((width, width), BF16), vm((width, width), BF16), vm((width, width), BF16), vm((width, width), BF16),
        vm((7, piece2, blk), F32), vm((7, piece2, blk), F32), vm(packed, F32),
        vm(packed, F32), vm((8, 128), F32),
        dma((nsteps,)), dma((2 * nsteps,)),
        dma((7,)), dma((7,)), dma((7,)), dma((7,)), dma((7,)), dma((7,)), dma((7,)), dma((7,)),
        dma((8,)), dma((8,)),
        dma((levels,)), dma((levels,)), dma((levels,)),
        dma((levels + 1,)), dma((levels + 1,)), dma((levels,)),
    ]
    vmem = pl.BlockSpec(memory_space=pltpu.VMEM)
    smem = pl.BlockSpec(memory_space=pltpu.SMEM)
    variances, schur = pl.pallas_call(
        functools.partial(kernel, ring, total_steps),
        out_shape=(jax.ShapeDtypeStruct((1, local), F32), jax.ShapeDtypeStruct((width, width), F32)),
        in_specs=[vmem, vmem, smem, smem],
        out_specs=(vmem, vmem),
        scratch_shapes=scratch,
        compiler_params=pltpu.CompilerParams(
            collective_id=0, has_side_effects=True, vmem_limit_bytes=56 * 1024 * 1024
        ),
        name="sweep",
    )(inv_diag[0].reshape(nodes // blk, blk, local), couple[0], col_blocks, row_blocks)
    return variances, schur[None]


def solution(mesh):
    return jax.shard_map(
        functools.partial(per_device, mesh.shape["panel"]),
        mesh=mesh,
        in_specs=(P("tm", None, "panel"), P("tm", None, None, None, None), P(), P("tm", None)),
        out_specs=(P("tm", "panel"), P("tm", None, None)),
        check_vma=False,
    )
```

```python
import functools

import jax
import jax.numpy as jnp
from jax import lax
from jax.experimental import pallas as pl
from jax.experimental.pallas import tpu as pltpu
from jax.sharding import PartitionSpec as P

MESH = pl.DeviceIdType.MESH
F32 = jnp.float32
BF16 = jnp.bfloat16

SPLIT = 1
ROUTES = (
    (
        (15, 0, 0, -1, 3, 0, 1), (26, 0, 0, 1, 23, 0, 1), (0, 0, 0, 0, 0, 0, 0), (1, 0, 0, 0, 1, 0, 0),
        (2, 0, 0, 0, 2, 0, 0), (3, 0, 0, 0, 3, 0, 0), (19, 0, 0, -1, 7, 0, 1), (4, 0, 0, 1, 8, 0, 1),
        (22, 0, 0, -1, 9, 0, 1), (6, 0, 0, 1, 11, 0, 1), (30, 0, 0, -1, 12, 0, 1), (7, 0, 0, 1, 14, 0, 1),
        (5, 0, 1, 0, 4, 0, 0), (23, 0, 0, -1, 14, 0, 1), (17, 0, 0, 1, 19, 0, 1), (8, 0, 1, 0, 5, 0, 0),
        (13, 0, 0, -1, 17, 0, 1), (18, 0, 0, 1, 22, 0, 1), (9, 0, 1, 0, 6, 0, 0), (29, 0, 0, -1, 20, 0, 1),
        (20, 0, 0, 1, 25, 0, 1), (10, 0, 1, 0, 7, 0, 0), (16, 0, 1, -1, 23, 0, 1), (25, 1, 0, 1, 26, 0, 1),
        (11, 0, 1, 0, 8, 0, 0), (12, 0, 0, -1, 26, 0, 1), (27, 0, 0, 1, 28, 0, 1), (21, 0, 1, -1, 28, 0, 1),
        (28, 1, 0, 1, 29, 0, 1), (14, 1, 1, 0, 9, 0, 0), (24, 1, 1, 0, 10, 0, 0), (31, 1, 1, 0, 11, 0, 0),
    ),
    (
        (12, 0, 0, 1, 4, 0, 1), (16, 0, 0, -1, 22, 0, 1), (13, 0, 0, 1, 12, 0, 1), (21, 0, 0, -1, 27, 0, 1),
        (29, 0, 0, 1, 14, 0, 1), (5, 0, 0, -1, 12, 0, 1), None, None,
        (4, 1, 0, 0, 0, 0, 0), (23, 0, 0, 1, 17, 0, 1), (8, 0, 1, -1, 15, 0, 1), (6, 1, 0, 0, 1, 0, 0),
        (22, 0, 0, 1, 19, 0, 1), (9, 0, 1, -1, 18, 0, 1), (7, 1, 0, 0, 2, 0, 0), (30, 0, 0, 1, 22, 0, 1),
        (10, 0, 1, -1, 21, 0, 1), (15, 0, 0, 1, 25, 0, 1), (11, 0, 1, -1, 24, 0, 1), (17, 1, 1, 0, 3, 0, 0),
        (19, 0, 0, 1, 26, 0, 1), (14, 0, 0, -1, 29, 0, 1), (18, 1, 1, 0, 4, 0, 0), (26, 1, 0, 1, 24, 0, 1),
        (24, 0, 1, -1, 30, 0, 1), (20, 1, 1, 0, 5, 0, 0), (25, 1, 0, 1, 27, 0, 1), (31, 0, 0, -1, 31, 0, 1),
        (27, 1, 1, 0, 6, 0, 0), (28, 1, 1, 0, 7, 0, 0), None, None,
    ),
    (
        (14, 0, 0, 1, 3, 0, 1), (8, 0, 0, -1, 10, 0, 1), (31, 0, 0, 1, 6, 0, 1), (9, 0, 0, -1, 13, 0, 1),
        (12, 1, 0, 1, 8, 0, 1), (10, 0, 0, -1, 16, 0, 1), None, (21, 0, 0, 1, 11, 0, 1),
        (11, 0, 0, -1, 18, 0, 1), (16, 0, 0, 1, 13, 0, 1), (24, 0, 0, -1, 24, 0, 1), None,
        (13, 1, 0, 1, 16, 0, 1), (17, 0, 1, -1, 19, 0, 1), (29, 1, 0, 1, 18, 0, 1), (18, 0, 1, -1, 22, 0, 1),
        None, (23, 1, 0, 1, 21, 0, 1), (20, 0, 1, -1, 25, 0, 1), (22, 1, 0, 1, 25, 0, 1),
        (27, 0, 1, -1, 28, 0, 1), None, (30, 1, 0, 1, 27, 0, 1), (28, 0, 1, -1, 29, 0, 1),
        (26, 1, 1, 0, 0, 0, 0), (15, 1, 1, 0, 1, 0, 0), (19, 1, 1, 0, 2, 0, 0), (25, 1, 1, 0, 3, 0, 0),
        None, None, None, None,
    ),
    (
        (24, 0, 0, 1, 3, 0, 1), (25, 0, 0, -1, 27, 0, 1), None, (14, 1, 0, 1, 8, 0, 1),
        (17, 0, 1, -1, 13, 0, 1), None, (31, 1, 0, 1, 10, 0, 1), (18, 0, 1, -1, 15, 0, 1),
        (12, 1, 0, 1, 13, 0, 1), (20, 0, 1, -1, 18, 0, 1), None, (21, 1, 0, 1, 16, 0, 1),
        (28, 0, 1, -1, 23, 0, 1), (16, 1, 0, 1, 17, 0, 1), (27, 0, 1, -1, 20, 0, 1), None,
        (13, 1, 0, 1, 21, 0, 1), (26, 0, 1, -1, 24, 0, 1), (29, 1, 0, 1, 22, 0, 1), (15, 0, 1, -1, 25, 0, 1),
        None, (23, 1, 0, 1, 25, 0, 1), (19, 0, 1, -1, 26, 0, 1), None,
        None, (22, 1, 1, 0, 0, 0, 0), None, (30, 1, 1, 0, 1, 0, 0),
        None, None, None, None,
    ),
    (
        (25, 0, 0, 1, 3, 0, 1), (17, 0, 0, -1, 4, 0, 1), (18, 0, 0, -1, 7, 0, 1), (24, 1, 0, 1, 8, 0, 1),
        (20, 0, 1, -1, 9, 0, 1), None, None, (28, 0, 1, -1, 12, 0, 1),
        (14, 1, 0, 1, 11, 0, 1), (27, 0, 1, -1, 14, 0, 1), (31, 1, 0, 1, 15, 0, 1), None,
        (26, 0, 1, -1, 17, 0, 1), (12, 1, 0, 1, 16, 0, 1), None, (15, 0, 1, -1, 19, 0, 1),
        (21, 1, 0, 1, 19, 0, 1), (16, 1, 0, 1, 21, 0, 1), (19, 0, 1, -1, 22, 0, 1), None,
        (22, 0, 1, -1, 25, 0, 1), (13, 1, 0, 1, 24, 0, 1), (29, 1, 0, 1, 26, 0, 1), (30, 0, 1, -1, 27, 0, 1),
        None, (23, 1, 1, 0, 0, 0, 0), None, None,
        None, None, None, None,
    ),
    (
        (20, 0, 0, -1, 4, 0, 1), None, (28, 0, 0, -1, 7, 0, 1), (25, 1, 0, 1, 8, 0, 1),
        (27, 0, 1, -1, 9, 0, 1), None, None, (26, 0, 1, -1, 12, 0, 1),
        (24, 1, 0, 1, 11, 0, 1), None, None, (14, 1, 0, 1, 15, 0, 1),
        (15, 0, 1, -1, 15, 0, 1), None, (19, 0, 1, -1, 18, 0, 1), (31, 1, 0, 1, 18, 0, 1),
        (12, 1, 0, 1, 20, 0, 1), (22, 0, 1, -1, 20, 0, 1), None, (21, 1, 0, 1, 23, 0, 1),
        (30, 0, 1, -1, 23, 0, 1), (16, 1, 0, 1, 25, 0, 1), (23, 0, 1, -1, 25, 0, 1), None,
        (13, 1, 1, 0, 0, 0, 0), None, (29, 1, 1, 0, 1, 0, 0), None,
        None, None, None, None,
    ),
    (
        (27, 0, 0, -1, 4, 0, 1), (28, 0, 0, 1, 4, 0, 1), (26, 0, 0, -1, 7, 0, 1), None,
        None, None, None, (15, 0, 1, -1, 12, 0, 1),
        (25, 1, 0, 1, 11, 0, 1), None, (19, 0, 1, -1, 14, 0, 1), (24, 1, 0, 1, 15, 0, 1),
        (22, 0, 1, -1, 17, 0, 1), None, None, (14, 1, 0, 1, 21, 0, 1),
        (30, 0, 1, -1, 20, 0, 1), (23, 0, 1, -1, 22, 0, 1), (31, 1, 0, 1, 24, 0, 1), None,
        (12, 1, 0, 1, 26, 0, 1), (13, 0, 1, -1, 24, 0, 1), (29, 0, 1, -1, 26, 0, 1), (21, 1, 0, 1, 28, 0, 1),
        None, (16, 1, 1, 0, 0, 0, 0), None, None,
        None, None, None, None,
    ),
    (
        None, None, None, (15, 0, 1, -1, 7, 0, 1),
        (28, 1, 0, 1, 28, 0, 1), None, None, (19, 0, 1, -1, 10, 0, 1),
        None, (22, 0, 1, -1, 12, 0, 1), None, (25, 1, 0, 1, 23, 0, 1),
        (30, 0, 1, -1, 16, 0, 1), None, (23, 0, 1, -1, 17, 0, 1), (24, 1, 0, 1, 30, 0, 1),
        None, (13, 0, 1, -1, 21, 0, 1), None, None,
        (29, 0, 1, -1, 22, 0, 1), (14, 1, 0, 1, 29, 0, 1), None, (16, 0, 1, -1, 25, 0, 1),
        (31, 1, 0, 1, 31, 0, 1), None, (12, 1, 1, 0, 0, 0, 0), None,
        (21, 1, 1, 0, 1, 0, 0), None, None, None,
    ),
)
LINK_AT = (0, 2, 4, 7, 10, 13, 15, 18, 20)
GRAM_AT = (
    (11, (0, 0, 0, 0, 0, 0, 0, 0), (2, 0, 0, 0, 0, 0, 0, 0)),
    (16, (2, 0, 0, 0, 0, 0, 0, 0), (3, 1, 0, 0, 0, 0, 0, 0)),
    (21, (3, 1, 0, 0, 0, 0, 0, 0), (3, 2, 0, 0, 0, 0, 0, 0)),
    (26, (3, 2, 0, 0, 0, 0, 0, 0), (4, 3, 1, 0, 0, 0, 0, 0)),
    (29, (4, 3, 1, 0, 0, 0, 0, 0), (4, 3, 2, 1, 0, 1, 0, 1)),
    (32, (4, 3, 2, 1, 0, 1, 0, 1), (6, 4, 2, 1, 1, 1, 1, 1)),
)
IDLE = (0, 0, 0, 0, 0, 0, 0)
PAIRS = ((0, 0), (0, 1), (0, 2), (1, 1), (1, 2), (2, 2))


def pick(me, values):
    values = [int(v) for v in values]
    if len(set(values)) == 1:
        return values[0]
    out = jnp.int32(values[-1])
    for p in range(len(values) - 1):
        out = jnp.where(me == p, jnp.int32(values[p]), out)
    return out


def when(cond):
    if isinstance(cond, (bool, int)):
        return (lambda f: f()) if cond else (lambda f: None)
    return pl.when(cond)


def dot(a, b):
    return jnp.dot(a, b, preferred_element_type=F32)


def split(x):
    high = x.astype(BF16)
    return high, (x - high.astype(F32)).astype(BF16)


def kernel(ring, total_steps, inv, couple, cols, rows, var_out, schur_out, spread, picks, squares,
           part, roots, got, link_part, link_full, link_put, link_got, keep_h, keep_l, keep_ht, keep_lt,
           b_put, b_got, a_now, a_put, a_got, mat_h, mat_l, tmp_h, tmp_l, last_got, last_full,
           state, state_full, send_sem, got_sem, lr_send, lr_recv, lg_send, lg_recv, fr_send, fr_recv,
           fg_send, fg_recv, st_send, st_recv, b_send, b_recv, br_send, a_send, a_recv, ar_send):
    me = lax.axis_index("panel")
    t = lax.axis_index("tm")
    m = t // 2
    core = lax.rem(t, 2)
    chips = total_steps // 2
    blk = couple.shape[2]
    local = inv.shape[2]
    width = 3 * blk
    half = blk // SPLIT
    nlocal = local // blk
    levels = len([d for d in (1, 2, 4, 8, 16) if d < chips])
    right = lax.rem(me + 1, ring)
    left = lax.rem(me + ring - 1, ring)
    mate = t + 1 - 2 * core

    def remote(src, dst, ssem, rsem, **where):
        return pltpu.make_async_remote_copy(src_ref=src, dst_ref=dst, send_sem=ssem, recv_sem=rsem,
                                            device_id=where, device_id_type=MESH)

    def arrived(dst, rsem):
        remote(dst, dst, rsem, rsem, tm=t, panel=me).wait_recv()

    def left_here(src, ssem):
        remote(src, src, ssem, ssem, tm=t, panel=me).wait_send()

    def mod(x):
        return lax.rem(x + 4 * ring, ring)

    barrier = pltpu.get_barrier_semaphore()
    greet = [(True, t, lax.rem(me + d, ring)) for d in range(1, ring)] + [(True, mate, me)]
    greet.append((jnp.logical_and(core == 1, t + 1 < total_steps), t + 1, me))
    greet.append((jnp.logical_and(core == 0, t > 0), t - 1, me))
    for k in range(levels):
        d = 2 ** k
        greet.append((jnp.logical_and(core == 0, m + d < chips), t + 2 * d, me))
        greet.append((jnp.logical_and(core == 0, m >= d), t - 2 * d, me))
    for cond, tt, pp in greet:
        @when(cond)
        def _(tt=tt, pp=pp):
            pl.semaphore_signal(barrier, inc=1, device_id=dict(tm=tt, panel=pp), device_id_type=MESH)

    for b in range(nlocal):
        for c in range(3):
            piece = jnp.zeros((blk, blk), F32)
            for k in range(4):
                off = rows[0, k] - (me * nlocal + b)
                piece = piece + couple[c, k].astype(F32) * (1 - jnp.minimum(off * off, 1)).astype(F32)
            spread[pl.ds(b * blk, blk), pl.ds(c * blk, blk)] = piece.astype(BF16)
    later = jnp.minimum(t + 1, total_steps - 1)
    for c in range(3):
        for n in range(SPLIT):
            picks[pl.ds(c * blk + n * half, half), :] = inv[SPLIT * cols[later, c] + n]
    for c in range(3):
        link_part[pl.ds(c * blk, blk), :] = dot(picks[pl.ds(c * blk, blk), :], spread[...])
    peers = jnp.int32(0)
    for cond, tt, pp in greet:
        peers = peers + (1 if cond is True else cond.astype(jnp.int32))
    pl.semaphore_wait(barrier, peers)

    def reduce_step(s, source, size, put, recv, ssem, rsem):
        for way in range(2):
            if s >= 4 - way:
                continue
            nbr = right if way == 0 else left
            r = mod(me + 4 - s) if way == 0 else mod(me - 3 + s)
            src = source.at[pl.ds(pl.multiple_of(r * size, 8), size), :]
            j = 4 * way + s
            if s > 0:
                arrived(recv.at[j - 1], rsem.at[j - 1])
                put[j] = src[...] + recv[j - 1]
                src = put.at[j]
            remote(src, recv.at[j], ssem.at[j], rsem.at[j], panel=nbr).start()

    def reduce_end(source, size, recv, rsem, dest):
        arrived(recv.at[3], rsem.at[3])
        arrived(recv.at[6], rsem.at[6])
        at = pl.ds(pl.multiple_of(me * size, 8), size)
        dest[at, :] = source[at, :] + recv[3] + recv[6]

    def gather_step(s, dest, size, ssem, rsem):
        for way in range(2):
            if s >= 4 - way:
                continue
            nbr = right if way == 0 else left
            r = mod(me - s) if way == 0 else mod(me + s)
            at = pl.ds(pl.multiple_of(r * size, 8), size)
            j = 4 * way + s
            if s > 0:
                arrived(dest.at[at, :], rsem.at[j - 1])
            remote(dest.at[at, :], dest.at[at, :], ssem.at[j], rsem.at[j], panel=nbr).start()

    def gather_end(dest, size, rsem):
        for way in range(2):
            r = mod(me - 4) if way == 0 else mod(me + 3)
            at = pl.ds(pl.multiple_of(r * size, 8), size)
            arrived(dest.at[at, :], rsem.at[3 + 3 * way])

    def spread_start(source, size, recv, ssem, rsem):
        for d in range(1, ring):
            r = lax.rem(me + d, ring)
            src = source.at[pl.ds(pl.multiple_of(r * size, 8), size), :]
            remote(src, recv.at[d - 1], ssem.at[d - 1], rsem.at[d - 1], panel=r).start()

    def spread_end(source, size, recv, rsem, dest):
        at = pl.ds(pl.multiple_of(me * size, 8), size)
        x = source[at, :]
        for d in range(1, ring):
            arrived(recv.at[d - 1], rsem.at[d - 1])
            x = x + recv[d - 1]
        dest[at, :] = x

    def share_start(dest, size, ssem, rsem):
        at = pl.ds(pl.multiple_of(me * size, 8), size)
        for d in range(1, ring):
            remote(dest.at[at, :], dest.at[at, :], ssem.at[d - 1], rsem.at[d - 1], panel=lax.rem(me + d, ring)).start()

    def share_end(dest, size, rsem, done):
        for d in (1, 7, 2, 6, 3, 5, 4):
            r = lax.rem(me + ring - d, ring)
            at = pl.ds(pl.multiple_of(r * size, 8), size)
            arrived(dest.at[at, :], rsem.at[d - 1])
            if done is not None:
                done(d, at)

    def halves(n):
        return [pl.ds(0, n // 2), pl.ds(n // 2, n // 2)]

    def ship(src, dst, ssem, rsem, n, h, **where):
        at = halves(src.shape[1])[h]
        remote(src.at[n, at, :], dst.at[n, at, :], ssem.at[n, h], rsem.at[n, h], **where).start()

    def landed(dst, rsem, n, h):
        arrived(dst.at[n, halves(dst.shape[1])[h], :], rsem.at[n, h])

    def shipped(src, ssem, n):
        for h in range(2):
            left_here(src.at[n, halves(src.shape[1])[h], :], ssem.at[n, h])

    def relay(buf, ssem, rsem, n):
        for h in range(2):
            landed(buf, rsem, n, h)
            @when(core == 0)
            def _(h=h):
                ship(buf, buf, ssem, rsem, n, h, tm=mate)

    def keep(v, x):
        h, l = split(x)
        keep_h[v] = h
        keep_l[v] = l
        xt = x.T
        h, l = split(xt)
        keep_ht[v] = h
        keep_lt[v] = l

    def times_kept(x, v):
        h, l = split(x)
        return dot(h, keep_h[v]) + dot(h, keep_l[v]) + dot(l, keep_h[v])

    def unpack(src, write):
        for n, (i, j) in enumerate(PAIRS):
            x = src[pl.ds(n * blk, blk), :]
            write(i, j, x)
            if i != j:
                write(j, i, x.T)

    def sandwich(src, v):
        def write(i, j, x):
            h, l = split(x)
            mat_h[pl.ds(i * blk, blk), pl.ds(j * blk, blk)] = h
            mat_l[pl.ds(i * blk, blk), pl.ds(j * blk, blk)] = l
        unpack(src, write)
        x = dot(mat_h[...], keep_h[v]) + dot(mat_h[...], keep_l[v]) + dot(mat_l[...], keep_h[v])
        h, l = split(x)
        tmp_h[...] = h
        tmp_l[...] = l
        n = 0
        for i in range(3):
            rows_i = pl.ds(i * blk, blk)
            cols_i = pl.ds(i * blk, width - i * blk)
            x = (dot(keep_ht[v, rows_i, :], tmp_h[:, cols_i]) + dot(keep_ht[v, rows_i, :], tmp_l[:, cols_i])
                 + dot(keep_lt[v, rows_i, :], tmp_h[:, cols_i]))
            for j in range(3 - i):
                at = pl.ds(n * blk, blk)
                a_now[at, :] = a_now[at, :] + x[:, j * blk:(j + 1) * blk]
                n += 1

    def add_squares(first, count):
        def one(n, total):
            x = inv[n].astype(F32)
            return total + jnp.sum((x * x).reshape(half // 8, 8, local), axis=0)
        squares[...] = lax.fori_loop(first, first + count, one, squares[...])

    def basis_step(i):
        acts = [ROUTES[p][i] for p in range(ring)]
        active = pick(me, [a is not None for a in acts])
        acts = [a or IDLE for a in acts]
        steps = got.shape[0] // 2

        @when(active == 1)
        def _():
            row = pick(me, [a[0] for a in acts])
            for side in range(2):
                @when(pick(me, [a[1 + side] for a in acts]) == 1)
                def _(side=side):
                    arrived(got.at[side * steps + i], got_sem.at[side * steps + i])
                    part[row] = part[row] + got[side * steps + i]
            slot = pick(me, [a[4] + (steps if a[3] < 0 else 0) for a in acts])

            @when(pick(me, [a[3] != 0 for a in acts]) == 1)
            def _():
                before = pick(me, [a[5] for a in acts])
                @when(before > 0)
                def _():
                    left_here(part.at[0], send_sem.at[before - 1])
                to = pick(me, [(p + acts[p][3]) % ring for p in range(ring)])
                remote(part.at[row], got.at[slot], send_sem.at[i], got_sem.at[slot], panel=to).start()

            @when(pick(me, [a[3] == 0 for a in acts]) == 1)
            def _():
                roots[pl.ds(pl.multiple_of(slot * half, half), half), :] = part[row]

    def add_gram(n, _):
        x = roots[pl.ds(pl.multiple_of(n * 2 * blk, 2 * blk), 2 * blk), :]
        h, l = split(x)
        th, tl = split(x.T)
        n = 0
        for b in range(3):
            at = slice(b * blk, (b + 1) * blk)
            y = dot(th[at], h[:, b * blk:]) + dot(th[at], l[:, b * blk:]) + dot(tl[at], h[:, b * blk:])
            for j in range(3 - b):
                at = pl.ds(n * blk, blk)
                a_now[at, :] = a_now[at, :] + y[:, j * blk:(j + 1) * blk]
                n += 1
        return 0

    def b_first():
        @when(core == 1)
        def _():
            b_put[0] = link_full[...]
            for h in range(2):
                ship(b_put, b_got, b_send, b_recv, 0, h, tm=mate)
        keep(0, link_full[...])

    def b_pair():
        @when(core == 0)
        def _():
            for h in range(2):
                landed(b_got, b_recv, 0, h)
            x = times_kept(b_got[0], 0)
            keep(1, x)
            if levels > 1:
                b_put[1] = x
        @when(core == 1)
        def _():
            keep_h[1] = keep_h[0]
            keep_l[1] = keep_l[0]
            keep_ht[1] = keep_ht[0]
            keep_lt[1] = keep_lt[0]

    def b_sends(k):
        d = 2 ** k
        return jnp.logical_and(core == 0, jnp.logical_and(m >= d, m + d < chips))

    def b_start(k):
        @when(b_sends(k))
        def _():
            for h in range(2):
                ship(b_put, b_got, b_send, b_recv, k + 1, h, tm=t - 2 ** (k + 1))

    def b_relays(k):
        return jnp.logical_and(core == 0, m + 2 ** (k + 1) < chips)

    def b_end(k, which):
        @when(jnp.logical_and(core == which, m + 2 ** (k + 1) < chips))
        def _():
            relay(b_got, br_send, b_recv, k + 1)
            x = times_kept(b_got[k + 1], k + 1)
            keep(k + 2, x)
            if which == 0 and k + 2 < levels:
                b_put[k + 2] = x

    def partial_rows(n, _):
        at = pl.ds(n * 4 * SPLIT, 4 * SPLIT)
        x = dot(inv[at].reshape(4 * blk, local), spread[...])
        part[at] = x.reshape(4 * SPLIT, half, width)
        return 0
    size = width // ring
    reduce_step(0, link_part, size, link_put, link_got, lr_send, lr_recv)
    lax.fori_loop(0, inv.shape[0] // (4 * SPLIT), partial_rows, 0)
    a_now[...] = jnp.zeros_like(a_now)
    roots[...] = jnp.zeros_like(roots)
    squares[...] = jnp.zeros_like(squares)
    nsteps = got.shape[0] // 2
    nblocks = inv.shape[0]
    extra = {}

    def add(i, f):
        extra.setdefault(i, []).append(f)

    for s in range(1, 4):
        add(LINK_AT[s], functools.partial(reduce_step, s, link_part, size, link_put, link_got, lr_send, lr_recv))
    add(LINK_AT[4], functools.partial(reduce_end, link_part, size, link_got, lr_recv, link_full))
    for s in range(4):
        add(LINK_AT[4 + s], functools.partial(gather_step, s, link_full, size, lg_send, lg_recv))
    first = LINK_AT[8]
    add(first, functools.partial(gather_end, link_full, size, lg_recv))
    add(first, b_first)
    add(first + 1, b_pair)
    if levels > 1:
        add(first + 1, functools.partial(b_start, 0))
        add(first + 6, functools.partial(b_end, 0, 0))
        add(first + 7, functools.partial(b_end, 0, 1))
    if levels > 2:
        add(first + 6, functools.partial(b_start, 1))
    for i, low, high in GRAM_AT:
        add(i, lambda low=low, high=high: lax.fori_loop(pick(me, low), pick(me, high), add_gram, 0))
    for i in range(max(nsteps, max(extra) + 1)):
        for f in extra.get(i, []):
            f()
        if i < nsteps:
            basis_step(i)

    @when(core == 1)
    def _():
        a_put[0] = a_now[...]
        for h in range(2):
            ship(a_put, a_got, a_send, a_recv, 0, h, tm=mate)

    @when(core == 0)
    def _():
        for h in range(2):
            landed(a_got, a_recv, 0, h)
        sandwich(a_got.at[0], 0)

    for k in range(levels):
        d = 2 ** k
        @when(jnp.logical_and(core == 0, m >= d))
        def _(k=k, d=d):
            a_put[k + 1] = a_now[...]
            for h in range(2):
                ship(a_put, a_got, a_send, a_recv, k + 1, h, tm=t - 2 * d)

        if 0 < k and k + 1 < levels:
            b_end(k, 0)
            if k + 2 < levels:
                b_start(k + 1)
        add_squares(k * nblocks // levels, nblocks // levels)

        @when(m + d < chips)
        def _(k=k):
            relay(a_got, ar_send, a_recv, k + 1)
            sandwich(a_got.at[k + 1], k + 1)
        if 0 < k and k + 1 < levels:
            b_end(k, 1)

    size2 = 6 * blk // ring

    def forward(j, at):
        @when(t > 0)
        def _():
            remote(last_full.at[at, :], state.at[at, :], st_send.at[j], st_recv.at[j], tm=t - 1).start()

    spread_start(a_now, size2, last_got, fr_send, fr_recv)
    spread_end(a_now, size2, last_got, fr_recv, last_full)
    share_start(last_full, size2, fg_send, fg_recv)
    forward(0, pl.ds(pl.multiple_of(me * size2, 8), size2))
    share_end(last_full, size2, fg_recv, forward)

    def write_schur(i, j, x):
        schur_out[pl.ds(i * blk, blk), pl.ds(j * blk, blk)] = x
    unpack(last_full, write_schur)

    @when(t + 1 < total_steps)
    def _():
        for d in range(ring):
            r = lax.rem(me + ring - d, ring)
            at = pl.ds(pl.multiple_of(r * size2, 8), size2)
            arrived(state.at[at, :], st_recv.at[d])

    @when(t + 1 == total_steps)
    def _():
        state[...] = jnp.zeros_like(state)

    def write_state(i, j, x):
        h, l = split(x)
        mat_h[pl.ds(i * blk, blk), pl.ds(j * blk, blk)] = h
        mat_l[pl.ds(i * blk, blk), pl.ds(j * blk, blk)] = l
    unpack(state, write_state)
    total = jnp.sum(squares[...], axis=0, keepdims=True)
    y = dot(mat_h[...], picks[...]) + dot(mat_l[...], picks[...])
    var_out[...] = total + jnp.sum(picks[...].astype(F32) * y, axis=0, keepdims=True)

    for i in range(nsteps):
        acts = [ROUTES[p][i] or IDLE for p in range(ring)]
        @when(pick(me, [a[6] for a in acts]) == 1)
        def _(i=i):
            left_here(part.at[0], send_sem.at[i])
    for j in range(ring - 1):
        left_here(link_got.at[j], lr_send.at[j])
        left_here(link_got.at[j], lg_send.at[j])
        left_here(last_got.at[j], fr_send.at[j])
        left_here(last_got.at[j], fg_send.at[j])

    @when(t > 0)
    def _():
        for j in range(ring):
            left_here(last_got.at[0], st_send.at[j])

    @when(core == 1)
    def _():
        shipped(b_got, b_send, 0)
        shipped(a_got, a_send, 0)
    for k in range(levels):
        d = 2 ** k
        if k < levels - 1:
            @when(b_sends(k))
            def _(k=k):
                shipped(b_got, b_send, k + 1)
            @when(b_relays(k))
            def _(k=k):
                shipped(b_got, br_send, k + 1)
        @when(jnp.logical_and(core == 0, m >= d))
        def _(k=k):
            shipped(a_got, a_send, k + 1)
        @when(jnp.logical_and(core == 0, m + d < chips))
        def _(k=k):
            shipped(a_got, ar_send, k + 1)


def per_device(ring, inv_diag, couple, col_blocks, row_blocks):
    nodes, local = inv_diag.shape[1], inv_diag.shape[2]
    blk = couple.shape[3]
    width = couple.shape[1] * blk
    total_steps = col_blocks.shape[0]
    chips = total_steps // 2
    levels = len([d for d in (1, 2, 4, 8, 16) if d < chips])
    nsteps = len(ROUTES[0])
    half = blk // SPLIT
    piece, piece2 = width // ring, 6 * blk // ring
    vm, dma = pltpu.VMEM, pltpu.SemaphoreType.DMA
    packed = (6 * blk, blk)
    scratch = [
        vm((local, width), BF16), vm((width, local), BF16), vm((8, local), F32),
        vm((nodes // half, half, width), F32), vm((2 * blk * max(GRAM_AT[-1][2]), width), F32), vm((2 * nsteps, half, width), F32),
        vm((width, width), F32), vm((width, width), F32), vm((7, piece, width), F32), vm((7, piece, width), F32),
        vm((levels + 1, width, width), BF16), vm((levels + 1, width, width), BF16),
        vm((levels + 1, width, width), BF16), vm((levels + 1, width, width), BF16),
        vm((levels, width, width), F32), vm((levels, width, width), F32),
        vm(packed, F32), vm((levels + 1,) + packed, F32), vm((levels + 1,) + packed, F32),
        vm((width, width), BF16), vm((width, width), BF16), vm((width, width), BF16), vm((width, width), BF16),
        vm((ring - 1, piece2, blk), F32), vm(packed, F32),
        vm(packed, F32), vm((8, 128), F32),
        dma((nsteps,)), dma((2 * nsteps,)),
        *[dma((ring - 1,)) for _ in range(8)],
        dma((ring,)), dma((ring,)),
        dma((levels, 2)), dma((levels, 2)), dma((levels, 2)),
        dma((levels + 1, 2)), dma((levels + 1, 2)), dma((levels + 1, 2)),
    ]
    vmem = pl.BlockSpec(memory_space=pltpu.VMEM)
    smem = pl.BlockSpec(memory_space=pltpu.SMEM)
    variances, schur = pl.pallas_call(
        functools.partial(kernel, ring, total_steps),
        out_shape=(jax.ShapeDtypeStruct((1, local), F32), jax.ShapeDtypeStruct((width, width), F32)),
        in_specs=[vmem, vmem, smem, smem],
        out_specs=(vmem, vmem),
        scratch_shapes=scratch,
        compiler_params=pltpu.CompilerParams(
            collective_id=0, has_side_effects=True, vmem_limit_bytes=56 * 1024 * 1024
        ),
        name="sweep",
    )(inv_diag[0].reshape(nodes // half, half, local), couple[0], col_blocks, row_blocks)
    return variances, schur[None]


def solution(mesh):
    return jax.shard_map(
        functools.partial(per_device, mesh.shape["panel"]),
        mesh=mesh,
        in_specs=(P("tm", None, "panel"), P("tm", None, None, None, None), P(), P("tm", None)),
        out_specs=(P("tm", "panel"), P("tm", None, None)),
        check_vma=False,
    )
```

```python
import functools

import jax
import jax.numpy as jnp
from jax import lax
from jax.experimental import pallas as pl
from jax.experimental.pallas import tpu as pltpu
from jax.sharding import PartitionSpec as P

MESH = pl.DeviceIdType.MESH
F32 = jnp.float32
BF16 = jnp.bfloat16

SPLIT = 1
ROUTES = (
    (
        (15, 0, 0, -1, 3, 0, 1), (26, 0, 0, 1, 23, 0, 1), (0, 0, 0, 0, 0, 0, 0), (1, 0, 0, 0, 1, 0, 0),
        (2, 0, 0, 0, 2, 0, 0), (3, 0, 0, 0, 3, 0, 0), (19, 0, 0, -1, 7, 0, 1), (4, 0, 0, 1, 8, 0, 1),
        (22, 0, 0, -1, 9, 0, 1), (6, 0, 0, 1, 11, 0, 1), (30, 0, 0, -1, 12, 0, 1), (7, 0, 0, 1, 14, 0, 1),
        (5, 0, 1, 0, 4, 0, 0), (23, 0, 0, -1, 14, 0, 1), (17, 0, 0, 1, 19, 0, 1), (8, 0, 1, 0, 5, 0, 0),
        (13, 0, 0, -1, 17, 0, 1), (18, 0, 0, 1, 22, 0, 1), (9, 0, 1, 0, 6, 0, 0), (29, 0, 0, -1, 20, 0, 1),
        (20, 0, 0, 1, 25, 0, 1), (10, 0, 1, 0, 7, 0, 0), (16, 0, 1, -1, 23, 0, 1), (25, 1, 0, 1, 26, 0, 1),
        (11, 0, 1, 0, 8, 0, 0), (12, 0, 0, -1, 26, 0, 1), (27, 0, 0, 1, 28, 0, 1), (21, 0, 1, -1, 28, 0, 1),
        (28, 1, 0, 1, 29, 0, 1), (14, 1, 1, 0, 9, 0, 0), (24, 1, 1, 0, 10, 0, 0), (31, 1, 1, 0, 11, 0, 0),
    ),
    (
        (12, 0, 0, 1, 4, 0, 1), (16, 0, 0, -1, 22, 0, 1), (13, 0, 0, 1, 12, 0, 1), (21, 0, 0, -1, 27, 0, 1),
        (29, 0, 0, 1, 14, 0, 1), (5, 0, 0, -1, 12, 0, 1), None, None,
        (4, 1, 0, 0, 0, 0, 0), (23, 0, 0, 1, 17, 0, 1), (8, 0, 1, -1, 15, 0, 1), (6, 1, 0, 0, 1, 0, 0),
        (22, 0, 0, 1, 19, 0, 1), (9, 0, 1, -1, 18, 0, 1), (7, 1, 0, 0, 2, 0, 0), (30, 0, 0, 1, 22, 0, 1),
        (10, 0, 1, -1, 21, 0, 1), (15, 0, 0, 1, 25, 0, 1), (11, 0, 1, -1, 24, 0, 1), (17, 1, 1, 0, 3, 0, 0),
        (19, 0, 0, 1, 26, 0, 1), (14, 0, 0, -1, 29, 0, 1), (18, 1, 1, 0, 4, 0, 0), (26, 1, 0, 1, 24, 0, 1),
        (24, 0, 1, -1, 30, 0, 1), (20, 1, 1, 0, 5, 0, 0), (25, 1, 0, 1, 27, 0, 1), (31, 0, 0, -1, 31, 0, 1),
        (27, 1, 1, 0, 6, 0, 0), (28, 1, 1, 0, 7, 0, 0), None, None,
    ),
    (
        (14, 0, 0, 1, 3, 0, 1), (8, 0, 0, -1, 10, 0, 1), (31, 0, 0, 1, 6, 0, 1), (9, 0, 0, -1, 13, 0, 1),
        (12, 1, 0, 1, 8, 0, 1), (10, 0, 0, -1, 16, 0, 1), None, (21, 0, 0, 1, 11, 0, 1),
        (11, 0, 0, -1, 18, 0, 1), (16, 0, 0, 1, 13, 0, 1), (24, 0, 0, -1, 24, 0, 1), None,
        (13, 1, 0, 1, 16, 0, 1), (17, 0, 1, -1, 19, 0, 1), (29, 1, 0, 1, 18, 0, 1), (18, 0, 1, -1, 22, 0, 1),
        None, (23, 1, 0, 1, 21, 0, 1), (20, 0, 1, -1, 25, 0, 1), (22, 1, 0, 1, 25, 0, 1),
        (27, 0, 1, -1, 28, 0, 1), None, (30, 1, 0, 1, 27, 0, 1), (28, 0, 1, -1, 29, 0, 1),
        (26, 1, 1, 0, 0, 0, 0), (15, 1, 1, 0, 1, 0, 0), (19, 1, 1, 0, 2, 0, 0), (25, 1, 1, 0, 3, 0, 0),
        None, None, None, None,
    ),
    (
        (24, 0, 0, 1, 3, 0, 1), (25, 0, 0, -1, 27, 0, 1), None, (14, 1, 0, 1, 8, 0, 1),
        (17, 0, 1, -1, 13, 0, 1), None, (31, 1, 0, 1, 10, 0, 1), (18, 0, 1, -1, 15, 0, 1),
        (12, 1, 0, 1, 13, 0, 1), (20, 0, 1, -1, 18, 0, 1), None, (21, 1, 0, 1, 16, 0, 1),
        (28, 0, 1, -1, 23, 0, 1), (16, 1, 0, 1, 17, 0, 1), (27, 0, 1, -1, 20, 0, 1), None,
        (13, 1, 0, 1, 21, 0, 1), (26, 0, 1, -1, 24, 0, 1), (29, 1, 0, 1, 22, 0, 1), (15, 0, 1, -1, 25, 0, 1),
        None, (23, 1, 0, 1, 25, 0, 1), (19, 0, 1, -1, 26, 0, 1), None,
        None, (22, 1, 1, 0, 0, 0, 0), None, (30, 1, 1, 0, 1, 0, 0),
        None, None, None, None,
    ),
    (
        (25, 0, 0, 1, 3, 0, 1), (17, 0, 0, -1, 4, 0, 1), (18, 0, 0, -1, 7, 0, 1), (24, 1, 0, 1, 8, 0, 1),
        (20, 0, 1, -1, 9, 0, 1), None, None, (28, 0, 1, -1, 12, 0, 1),
        (14, 1, 0, 1, 11, 0, 1), (27, 0, 1, -1, 14, 0, 1), (31, 1, 0, 1, 15, 0, 1), None,
        (26, 0, 1, -1, 17, 0, 1), (12, 1, 0, 1, 16, 0, 1), None, (15, 0, 1, -1, 19, 0, 1),
        (21, 1, 0, 1, 19, 0, 1), (16, 1, 0, 1, 21, 0, 1), (19, 0, 1, -1, 22, 0, 1), None,
        (22, 0, 1, -1, 25, 0, 1), (13, 1, 0, 1, 24, 0, 1), (29, 1, 0, 1, 26, 0, 1), (30, 0, 1, -1, 27, 0, 1),
        None, (23, 1, 1, 0, 0, 0, 0), None, None,
        None, None, None, None,
    ),
    (
        (20, 0, 0, -1, 4, 0, 1), None, (28, 0, 0, -1, 7, 0, 1), (25, 1, 0, 1, 8, 0, 1),
        (27, 0, 1, -1, 9, 0, 1), None, None, (26, 0, 1, -1, 12, 0, 1),
        (24, 1, 0, 1, 11, 0, 1), None, None, (14, 1, 0, 1, 15, 0, 1),
        (15, 0, 1, -1, 15, 0, 1), None, (19, 0, 1, -1, 18, 0, 1), (31, 1, 0, 1, 18, 0, 1),
        (12, 1, 0, 1, 20, 0, 1), (22, 0, 1, -1, 20, 0, 1), None, (21, 1, 0, 1, 23, 0, 1),
        (30, 0, 1, -1, 23, 0, 1), (16, 1, 0, 1, 25, 0, 1), (23, 0, 1, -1, 25, 0, 1), None,
        (13, 1, 1, 0, 0, 0, 0), None, (29, 1, 1, 0, 1, 0, 0), None,
        None, None, None, None,
    ),
    (
        (27, 0, 0, -1, 4, 0, 1), (28, 0, 0, 1, 4, 0, 1), (26, 0, 0, -1, 7, 0, 1), None,
        None, None, None, (15, 0, 1, -1, 12, 0, 1),
        (25, 1, 0, 1, 11, 0, 1), None, (19, 0, 1, -1, 14, 0, 1), (24, 1, 0, 1, 15, 0, 1),
        (22, 0, 1, -1, 17, 0, 1), None, None, (14, 1, 0, 1, 21, 0, 1),
        (30, 0, 1, -1, 20, 0, 1), (23, 0, 1, -1, 22, 0, 1), (31, 1, 0, 1, 24, 0, 1), None,
        (12, 1, 0, 1, 26, 0, 1), (13, 0, 1, -1, 24, 0, 1), (29, 0, 1, -1, 26, 0, 1), (21, 1, 0, 1, 28, 0, 1),
        None, (16, 1, 1, 0, 0, 0, 0), None, None,
        None, None, None, None,
    ),
    (
        None, None, None, (15, 0, 1, -1, 7, 0, 1),
        (28, 1, 0, 1, 28, 0, 1), None, None, (19, 0, 1, -1, 10, 0, 1),
        None, (22, 0, 1, -1, 12, 0, 1), None, (25, 1, 0, 1, 23, 0, 1),
        (30, 0, 1, -1, 16, 0, 1), None, (23, 0, 1, -1, 17, 0, 1), (24, 1, 0, 1, 30, 0, 1),
        None, (13, 0, 1, -1, 21, 0, 1), None, None,
        (29, 0, 1, -1, 22, 0, 1), (14, 1, 0, 1, 29, 0, 1), None, (16, 0, 1, -1, 25, 0, 1),
        (31, 1, 0, 1, 31, 0, 1), None, (12, 1, 1, 0, 0, 0, 0), None,
        (21, 1, 1, 0, 1, 0, 0), None, None, None,
    ),
)
LINK_AT = (0, 2, 4, 7, 10, 13, 15, 18, 20)
GRAM_AT = (
    (11, (0, 0, 0, 0, 0, 0, 0, 0), (2, 0, 0, 0, 0, 0, 0, 0)),
    (16, (2, 0, 0, 0, 0, 0, 0, 0), (3, 1, 0, 0, 0, 0, 0, 0)),
    (21, (3, 1, 0, 0, 0, 0, 0, 0), (3, 2, 0, 0, 0, 0, 0, 0)),
    (26, (3, 2, 0, 0, 0, 0, 0, 0), (4, 3, 1, 0, 0, 0, 0, 0)),
    (29, (4, 3, 1, 0, 0, 0, 0, 0), (4, 3, 2, 1, 0, 1, 0, 1)),
    (31, (4, 3, 2, 1, 0, 1, 0, 1), (5, 4, 2, 1, 0, 1, 0, 1)),
    (32, (5, 4, 2, 1, 0, 1, 0, 1), (6, 4, 2, 1, 1, 1, 1, 1)),
)
IDLE = (0, 0, 0, 0, 0, 0, 0)
PAIRS = ((0, 0), (0, 1), (0, 2), (1, 1), (1, 2), (2, 2))


def pick(me, values):
    values = [int(v) for v in values]
    if len(set(values)) == 1:
        return values[0]
    out = jnp.int32(values[-1])
    for p in range(len(values) - 1):
        out = jnp.where(me == p, jnp.int32(values[p]), out)
    return out


def when(cond):
    if isinstance(cond, (bool, int)):
        return (lambda f: f()) if cond else (lambda f: None)
    return pl.when(cond)


def dot(a, b):
    return jnp.dot(a, b, preferred_element_type=F32)


def split(x):
    high = x.astype(BF16)
    return high, (x - high.astype(F32)).astype(BF16)


def kernel(ring, total_steps, inv, couple, cols, rows, var_out, last_full, spread, picks, squares,
           part, roots, got, link_part, link_full, link_put, link_got, keep_h, keep_l, keep_ht, keep_lt,
           b_put, b_got, a_now, a_put, a_got, mat_h, mat_l, tmp_h, tmp_l, last_got,
           state, send_sem, got_sem, lr_send, lr_recv, lg_send, lg_recv, fr_send, fr_recv,
           fg_send, fg_recv, st_send, st_recv, b_send, b_recv, br_send, a_send, a_recv, ar_send):
    me = lax.axis_index("panel")
    t = lax.axis_index("tm")
    m = t // 2
    core = lax.rem(t, 2)
    chips = total_steps // 2
    blk = couple.shape[2]
    local = inv.shape[2]
    width = 3 * blk
    half = blk // SPLIT
    nlocal = local // blk
    levels = len([d for d in (1, 2, 4, 8, 16) if d < chips])
    right = lax.rem(me + 1, ring)
    left = lax.rem(me + ring - 1, ring)
    mate = t + 1 - 2 * core

    def remote(src, dst, ssem, rsem, **where):
        return pltpu.make_async_remote_copy(src_ref=src, dst_ref=dst, send_sem=ssem, recv_sem=rsem,
                                            device_id=where, device_id_type=MESH)

    def arrived(dst, rsem):
        remote(dst, dst, rsem, rsem, tm=t, panel=me).wait_recv()

    def left_here(src, ssem):
        remote(src, src, ssem, ssem, tm=t, panel=me).wait_send()

    def mod(x):
        return lax.rem(x + 4 * ring, ring)

    barrier = pltpu.get_barrier_semaphore()
    greet = [(True, t, lax.rem(me + d, ring)) for d in range(1, ring)] + [(True, mate, me)]
    greet.append((jnp.logical_and(core == 1, t + 1 < total_steps), t + 1, me))
    greet.append((jnp.logical_and(core == 0, t > 0), t - 1, me))
    for k in range(levels):
        d = 2 ** k
        greet.append((jnp.logical_and(core == 0, m + d < chips), t + 2 * d, me))
        greet.append((jnp.logical_and(core == 0, m >= d), t - 2 * d, me))
    for cond, tt, pp in greet:
        @when(cond)
        def _(tt=tt, pp=pp):
            pl.semaphore_signal(barrier, inc=1, device_id=dict(tm=tt, panel=pp), device_id_type=MESH)

    for b in range(nlocal):
        for c in range(3):
            piece = jnp.zeros((blk, blk), F32)
            for k in range(4):
                off = rows[0, k] - (me * nlocal + b)
                piece = piece + couple[c, k].astype(F32) * (1 - jnp.minimum(off * off, 1)).astype(F32)
            spread[pl.ds(b * blk, blk), pl.ds(c * blk, blk)] = piece.astype(BF16)
    later = jnp.minimum(t + 1, total_steps - 1)
    for c in range(3):
        for n in range(SPLIT):
            picks[pl.ds(c * blk + n * half, half), :] = inv[SPLIT * cols[later, c] + n]
    for c in range(3):
        link_part[pl.ds(c * blk, blk), :] = dot(picks[pl.ds(c * blk, blk), :], spread[...])
    peers = jnp.int32(0)
    for cond, tt, pp in greet:
        peers = peers + (1 if cond is True else cond.astype(jnp.int32))
    pl.semaphore_wait(barrier, peers)

    def reduce_step(s, source, size, put, recv, ssem, rsem):
        for way in range(2):
            if s >= 4 - way:
                continue
            nbr = right if way == 0 else left
            r = mod(me + 4 - s) if way == 0 else mod(me - 3 + s)
            src = source.at[pl.ds(pl.multiple_of(r * size, 8), size), :]
            j = 4 * way + s
            if s > 0:
                arrived(recv.at[j - 1], rsem.at[j - 1])
                put[j] = src[...] + recv[j - 1]
                src = put.at[j]
            remote(src, recv.at[j], ssem.at[j], rsem.at[j], panel=nbr).start()

    def reduce_end(source, size, recv, rsem, dest):
        arrived(recv.at[3], rsem.at[3])
        arrived(recv.at[6], rsem.at[6])
        at = pl.ds(pl.multiple_of(me * size, 8), size)
        dest[at, :] = source[at, :] + recv[3] + recv[6]

    def gather_step(s, dest, size, ssem, rsem):
        for way in range(2):
            if s >= 4 - way:
                continue
            nbr = right if way == 0 else left
            r = mod(me - s) if way == 0 else mod(me + s)
            at = pl.ds(pl.multiple_of(r * size, 8), size)
            j = 4 * way + s
            if s > 0:
                arrived(dest.at[at, :], rsem.at[j - 1])
            remote(dest.at[at, :], dest.at[at, :], ssem.at[j], rsem.at[j], panel=nbr).start()

    def gather_end(dest, size, rsem):
        for way in range(2):
            r = mod(me - 4) if way == 0 else mod(me + 3)
            at = pl.ds(pl.multiple_of(r * size, 8), size)
            arrived(dest.at[at, :], rsem.at[3 + 3 * way])

    def spread_start(source, size, recv, ssem, rsem):
        for d in (4, 3, 5, 2, 6, 1, 7):
            r = lax.rem(me + d, ring)
            src = source.at[pl.ds(pl.multiple_of(r * size, 8), size), :]
            remote(src, recv.at[d - 1], ssem.at[d - 1], rsem.at[d - 1], panel=r).start()

    def spread_end(source, size, recv, rsem, dest):
        at = pl.ds(pl.multiple_of(me * size, 8), size)
        x = source[at, :]
        for d in range(1, ring):
            arrived(recv.at[d - 1], rsem.at[d - 1])
            x = x + recv[d - 1]
        dest[at, :] = x

    def share_start(dest, size, ssem, rsem):
        at = pl.ds(pl.multiple_of(me * size, 8), size)
        for d in range(1, ring):
            remote(dest.at[at, :], dest.at[at, :], ssem.at[d - 1], rsem.at[d - 1], panel=lax.rem(me + d, ring)).start()

    def share_end(dest, size, rsem, done):
        for d in (1, 7, 2, 6, 3, 5, 4):
            r = lax.rem(me + ring - d, ring)
            at = pl.ds(pl.multiple_of(r * size, 8), size)
            arrived(dest.at[at, :], rsem.at[d - 1])
            if done is not None:
                done(d, at)

    def halves(n):
        return [pl.ds(0, n // 2), pl.ds(n // 2, n // 2)]

    def ship(src, dst, ssem, rsem, n, h, **where):
        at = halves(src.shape[1])[h]
        remote(src.at[n, at, :], dst.at[n, at, :], ssem.at[n, h], rsem.at[n, h], **where).start()

    def landed(dst, rsem, n, h):
        arrived(dst.at[n, halves(dst.shape[1])[h], :], rsem.at[n, h])

    def shipped(src, ssem, n):
        for h in range(2):
            left_here(src.at[n, halves(src.shape[1])[h], :], ssem.at[n, h])

    def relay(buf, ssem, rsem, n, then=None):
        for h in range(2):
            landed(buf, rsem, n, h)
            @when(core == 0)
            def _(h=h):
                ship(buf, buf, ssem, rsem, n, h, tm=mate)
            if then is not None:
                then(h)

    def sandwich_half(n, v, h):
        if h == 0:
            sandwich(a_got.at[n], v, 0, range(3), 0, blk)
        else:
            sandwich(a_got.at[n], v, 1, range(3, 6), blk, 2 * blk)

    def keep(v, x):
        h, l = split(x)
        keep_h[v] = h
        keep_l[v] = l
        xt = x.T
        h, l = split(xt)
        keep_ht[v] = h
        keep_lt[v] = l

    def times_kept(x, v):
        h, l = split(x)
        return dot(h, keep_h[v]) + dot(h, keep_l[v]) + dot(l, keep_h[v])

    def unpack(src, write, blocks=range(6)):
        for n in blocks:
            i, j = PAIRS[n]
            x = src[pl.ds(n * blk, blk), :]
            write(i, j, x)
            if i != j:
                write(j, i, x.T)

    def sandwich(src, v, part, blocks, top, count):
        def write(i, j, x):
            h, l = split(x)
            mat_h[pl.ds(i * blk, blk), pl.ds(j * blk, blk)] = h
            mat_l[pl.ds(i * blk, blk), pl.ds(j * blk, blk)] = l
        unpack(src, write, blocks)
        at = pl.ds(top, count)
        x = dot(mat_h[at, :], keep_h[v]) + dot(mat_h[at, :], keep_l[v]) + dot(mat_l[at, :], keep_h[v])
        h, l = split(x)
        tmp_h[at, :] = h
        tmp_l[at, :] = l
        if part == 0:
            return
        n = 0
        for i in range(3):
            rows_i = pl.ds(i * blk, blk)
            cols_i = pl.ds(i * blk, width - i * blk)
            x = (dot(keep_ht[v, rows_i, :], tmp_h[:, cols_i]) + dot(keep_ht[v, rows_i, :], tmp_l[:, cols_i])
                 + dot(keep_lt[v, rows_i, :], tmp_h[:, cols_i]))
            for j in range(3 - i):
                at = pl.ds(n * blk, blk)
                a_now[at, :] = a_now[at, :] + x[:, j * blk:(j + 1) * blk]
                n += 1

    def add_squares(first, count):
        def one(n, total):
            x = inv[n].astype(F32)
            return total + jnp.sum((x * x).reshape(half // 8, 8, local), axis=0)
        squares[...] = lax.fori_loop(first, first + count, one, squares[...])

    def basis_step(i):
        acts = [ROUTES[p][i] for p in range(ring)]
        active = pick(me, [a is not None for a in acts])
        acts = [a or IDLE for a in acts]
        steps = got.shape[0] // 2

        @when(active == 1)
        def _():
            row = pick(me, [a[0] for a in acts])
            for side in range(2):
                @when(pick(me, [a[1 + side] for a in acts]) == 1)
                def _(side=side):
                    arrived(got.at[side * steps + i], got_sem.at[side * steps + i])
                    part[row] = part[row] + got[side * steps + i]
            slot = pick(me, [a[4] + (steps if a[3] < 0 else 0) for a in acts])

            @when(pick(me, [a[3] != 0 for a in acts]) == 1)
            def _():
                before = pick(me, [a[5] for a in acts])
                @when(before > 0)
                def _():
                    left_here(part.at[0], send_sem.at[before - 1])
                to = pick(me, [(p + acts[p][3]) % ring for p in range(ring)])
                remote(part.at[row], got.at[slot], send_sem.at[i], got_sem.at[slot], panel=to).start()

            @when(pick(me, [a[3] == 0 for a in acts]) == 1)
            def _():
                roots[pl.ds(pl.multiple_of(slot * half, half), half), :] = part[row]

    def add_gram(n, _):
        x = roots[pl.ds(pl.multiple_of(n * 2 * blk, 2 * blk), 2 * blk), :]
        h, l = split(x)
        th, tl = split(x.T)
        n = 0
        for b in range(3):
            at = slice(b * blk, (b + 1) * blk)
            y = dot(th[at], h[:, b * blk:]) + dot(th[at], l[:, b * blk:]) + dot(tl[at], h[:, b * blk:])
            for j in range(3 - b):
                at = pl.ds(n * blk, blk)
                a_now[at, :] = a_now[at, :] + y[:, j * blk:(j + 1) * blk]
                n += 1
        return 0

    def b_first():
        @when(core == 1)
        def _():
            b_put[0] = link_full[...]
            for h in range(2):
                ship(b_put, b_got, b_send, b_recv, 0, h, tm=mate)
        keep(0, link_full[...])

    def b_pair():
        @when(core == 0)
        def _():
            for h in range(2):
                landed(b_got, b_recv, 0, h)
            x = times_kept(b_got[0], 0)
            keep(1, x)
            if levels > 1:
                b_put[1] = x
        @when(core == 1)
        def _():
            keep_h[1] = keep_h[0]
            keep_l[1] = keep_l[0]
            keep_ht[1] = keep_ht[0]
            keep_lt[1] = keep_lt[0]

    def b_sends(k):
        d = 2 ** k
        return jnp.logical_and(core == 0, jnp.logical_and(m >= d, m + d < chips))

    def b_start(k):
        @when(b_sends(k))
        def _():
            for h in range(2):
                ship(b_put, b_got, b_send, b_recv, k + 1, h, tm=t - 2 ** (k + 1))

    def b_relays(k):
        return jnp.logical_and(core == 0, m + 2 ** (k + 1) < chips)

    def b_end(k, which):
        @when(jnp.logical_and(core == which, m + 2 ** (k + 1) < chips))
        def _():
            relay(b_got, br_send, b_recv, k + 1)
            x = times_kept(b_got[k + 1], k + 1)
            keep(k + 2, x)
            if which == 0 and k + 2 < levels:
                b_put[k + 2] = x

    def partial_rows(n, _):
        at = pl.ds(n * 4 * SPLIT, 4 * SPLIT)
        x = dot(inv[at].reshape(4 * blk, local), spread[...])
        part[at] = x.reshape(4 * SPLIT, half, width)
        return 0
    size = width // ring
    reduce_step(0, link_part, size, link_put, link_got, lr_send, lr_recv)
    lax.fori_loop(0, inv.shape[0] // (4 * SPLIT), partial_rows, 0)
    a_now[...] = jnp.zeros_like(a_now)
    roots[...] = jnp.zeros_like(roots)
    squares[...] = jnp.zeros_like(squares)
    nsteps = got.shape[0] // 2
    nblocks = inv.shape[0]
    extra = {}

    def add(i, f):
        extra.setdefault(i, []).append(f)

    for s in range(1, 4):
        add(LINK_AT[s], functools.partial(reduce_step, s, link_part, size, link_put, link_got, lr_send, lr_recv))
    add(LINK_AT[4], functools.partial(reduce_end, link_part, size, link_got, lr_recv, link_full))
    for s in range(4):
        add(LINK_AT[4 + s], functools.partial(gather_step, s, link_full, size, lg_send, lg_recv))
    first = LINK_AT[8]
    add(first, functools.partial(gather_end, link_full, size, lg_recv))
    add(first, b_first)
    add(first + 1, b_pair)
    if levels > 1:
        add(first + 1, functools.partial(b_start, 0))
        add(first + 6, functools.partial(b_end, 0, 0))
        add(first + 7, functools.partial(b_end, 0, 1))
    if levels > 2:
        add(first + 6, functools.partial(b_start, 1))
    for i, low, high in GRAM_AT:
        add(i, lambda low=low, high=high: lax.fori_loop(pick(me, low), pick(me, high), add_gram, 0))
    for i in range(max(nsteps, max(extra) + 1)):
        for f in extra.get(i, []):
            f()
        if i < nsteps:
            basis_step(i)

    @when(core == 1)
    def _():
        a_put[0] = a_now[...]
        for h in range(2):
            ship(a_put, a_got, a_send, a_recv, 0, h, tm=mate)

    @when(core == 0)
    def _():
        for h in range(2):
            landed(a_got, a_recv, 0, h)
            sandwich_half(0, 0, h)

    for k in range(levels):
        d = 2 ** k
        @when(jnp.logical_and(core == 0, m >= d))
        def _(k=k, d=d):
            a_put[k + 1] = a_now[...]
            for h in range(2):
                ship(a_put, a_got, a_send, a_recv, k + 1, h, tm=t - 2 * d)

        if 0 < k and k + 1 < levels:
            b_end(k, 0)
            if k + 2 < levels:
                b_start(k + 1)
        add_squares(k * nblocks // levels, nblocks // levels)

        @when(m + d < chips)
        def _(k=k):
            relay(a_got, ar_send, a_recv, k + 1, functools.partial(sandwich_half, k + 1, k + 1))
        if 0 < k and k + 1 < levels:
            b_end(k, 1)

    size2 = 6 * blk // ring

    def forward(j, at):
        @when(t > 0)
        def _():
            remote(last_full.at[at, :], state.at[at, :], st_send.at[j], st_recv.at[j], tm=t - 1).start()

    spread_start(a_now, size2, last_got, fr_send, fr_recv)
    spread_end(a_now, size2, last_got, fr_recv, last_full)
    share_start(last_full, size2, fg_send, fg_recv)
    forward(0, pl.ds(pl.multiple_of(me * size2, 8), size2))
    share_end(last_full, size2, fg_recv, forward)

    @when(t + 1 < total_steps)
    def _():
        for d in range(ring):
            r = lax.rem(me + ring - d, ring)
            at = pl.ds(pl.multiple_of(r * size2, 8), size2)
            arrived(state.at[at, :], st_recv.at[d])

    @when(t + 1 == total_steps)
    def _():
        state[...] = jnp.zeros_like(state)

    def write_state(i, j, x):
        h, l = split(x)
        mat_h[pl.ds(i * blk, blk), pl.ds(j * blk, blk)] = h
        mat_l[pl.ds(i * blk, blk), pl.ds(j * blk, blk)] = l
    unpack(state, write_state)
    total = jnp.sum(squares[...], axis=0, keepdims=True)
    y = dot(mat_h[...], picks[...]) + dot(mat_l[...], picks[...])
    var_out[...] = total + jnp.sum(picks[...].astype(F32) * y, axis=0, keepdims=True)

    for i in range(nsteps):
        acts = [ROUTES[p][i] or IDLE for p in range(ring)]
        @when(pick(me, [a[6] for a in acts]) == 1)
        def _(i=i):
            left_here(part.at[0], send_sem.at[i])
    for j in range(ring - 1):
        left_here(link_got.at[j], lr_send.at[j])
        left_here(link_got.at[j], lg_send.at[j])
        left_here(last_got.at[j], fr_send.at[j])
        left_here(last_got.at[j], fg_send.at[j])

    @when(t > 0)
    def _():
        for j in range(ring):
            left_here(last_got.at[0], st_send.at[j])

    @when(core == 1)
    def _():
        shipped(b_got, b_send, 0)
        shipped(a_got, a_send, 0)
    for k in range(levels):
        d = 2 ** k
        if k < levels - 1:
            @when(b_sends(k))
            def _(k=k):
                shipped(b_got, b_send, k + 1)
            @when(b_relays(k))
            def _(k=k):
                shipped(b_got, br_send, k + 1)
        @when(jnp.logical_and(core == 0, m >= d))
        def _(k=k):
            shipped(a_got, a_send, k + 1)
        @when(jnp.logical_and(core == 0, m + d < chips))
        def _(k=k):
            shipped(a_got, ar_send, k + 1)


def finish(var, last, var_out, schur_out):
    blk = last.shape[1]
    var_out[...] = var[...]
    for n, (i, j) in enumerate(PAIRS):
        x = last[pl.ds(n * blk, blk), :]
        schur_out[pl.ds(i * blk, blk), pl.ds(j * blk, blk)] = x
        if i != j:
            schur_out[pl.ds(j * blk, blk), pl.ds(i * blk, blk)] = x.T


def per_device(ring, inv_diag, couple, col_blocks, row_blocks):
    nodes, local = inv_diag.shape[1], inv_diag.shape[2]
    blk = couple.shape[3]
    width = couple.shape[1] * blk
    total_steps = col_blocks.shape[0]
    chips = total_steps // 2
    levels = len([d for d in (1, 2, 4, 8, 16) if d < chips])
    nsteps = len(ROUTES[0])
    half = blk // SPLIT
    piece, piece2 = width // ring, 6 * blk // ring
    vm, dma = pltpu.VMEM, pltpu.SemaphoreType.DMA
    packed = (6 * blk, blk)
    scratch = [
        vm((local, width), BF16), vm((width, local), BF16), vm((8, local), F32),
        vm((nodes // half, half, width), F32), vm((2 * blk * max(GRAM_AT[-1][2]), width), F32), vm((2 * nsteps, half, width), F32),
        vm((width, width), F32), vm((width, width), F32), vm((7, piece, width), F32), vm((7, piece, width), F32),
        vm((levels + 1, width, width), BF16), vm((levels + 1, width, width), BF16),
        vm((levels + 1, width, width), BF16), vm((levels + 1, width, width), BF16),
        vm((levels, width, width), F32), vm((levels, width, width), F32),
        vm(packed, F32), vm((levels + 1,) + packed, F32), vm((levels + 1,) + packed, F32),
        vm((width, width), BF16), vm((width, width), BF16), vm((width, width), BF16), vm((width, width), BF16),
        vm((ring - 1, piece2, blk), F32),
        vm(packed, F32),
        dma((nsteps,)), dma((2 * nsteps,)),
        *[dma((ring - 1,)) for _ in range(8)],
        dma((ring,)), dma((ring,)),
        dma((levels, 2)), dma((levels, 2)), dma((levels, 2)),
        dma((levels + 1, 2)), dma((levels + 1, 2)), dma((levels + 1, 2)),
    ]
    vmem = pl.BlockSpec(memory_space=pltpu.VMEM)
    smem = pl.BlockSpec(memory_space=pltpu.SMEM)
    variances, last = pl.pallas_call(
        functools.partial(kernel, ring, total_steps),
        out_shape=(jax.ShapeDtypeStruct((1, local), F32), jax.ShapeDtypeStruct(packed, F32)),
        in_specs=[vmem, vmem, smem, smem],
        out_specs=(vmem, vmem),
        scratch_shapes=scratch,
        compiler_params=pltpu.CompilerParams(
            collective_id=0, has_side_effects=True, vmem_limit_bytes=56 * 1024 * 1024
        ),
        name="sweep",
    )(inv_diag[0].reshape(nodes // half, half, local), couple[0], col_blocks, row_blocks)
    variances, schur = pl.pallas_call(
        finish,
        out_shape=(jax.ShapeDtypeStruct((1, local), F32), jax.ShapeDtypeStruct((width, width), F32)),
        in_specs=[vmem, vmem],
        out_specs=(vmem, vmem),
        name="finish",
    )(variances, last)
    return variances, schur[None]


def solution(mesh):
    return jax.shard_map(
        functools.partial(per_device, mesh.shape["panel"]),
        mesh=mesh,
        in_specs=(P("tm", None, "panel"), P("tm", None, None, None, None), P(), P("tm", None)),
        out_specs=(P("tm", "panel"), P("tm", None, None)),
        check_vma=False,
    )
```

```python
import functools

import jax
import jax.numpy as jnp
from jax import lax
from jax.experimental import pallas as pl
from jax.experimental.pallas import tpu as pltpu
from jax.sharding import PartitionSpec as P

MESH = pl.DeviceIdType.MESH
F32 = jnp.float32
BF16 = jnp.bfloat16

SPLIT = 1
ROUTES = (
    (
        (15, 0, 0, -1, 3, 0, 1), (26, 0, 0, 1, 23, 0, 1), (0, 0, 0, 0, 0, 0, 0), (1, 0, 0, 0, 1, 0, 0),
        (2, 0, 0, 0, 2, 0, 0), (3, 0, 0, 0, 3, 0, 0), (19, 0, 0, -1, 7, 0, 1), (4, 0, 0, 1, 8, 0, 1),
        (22, 0, 0, -1, 9, 0, 1), (6, 0, 0, 1, 11, 0, 1), (30, 0, 0, -1, 12, 0, 1), (7, 0, 0, 1, 14, 0, 1),
        (5, 0, 1, 0, 4, 0, 0), (23, 0, 0, -1, 14, 0, 1), (17, 0, 0, 1, 19, 0, 1), (8, 0, 1, 0, 5, 0, 0),
        (13, 0, 0, -1, 17, 0, 1), (18, 0, 0, 1, 22, 0, 1), (9, 0, 1, 0, 6, 0, 0), (29, 0, 0, -1, 20, 0, 1),
        (20, 0, 0, 1, 25, 0, 1), (10, 0, 1, 0, 7, 0, 0), (16, 0, 1, -1, 23, 0, 1), (25, 1, 0, 1, 26, 0, 1),
        (11, 0, 1, 0, 8, 0, 0), (12, 0, 0, -1, 26, 0, 1), (27, 0, 0, 1, 28, 0, 1), (21, 0, 1, -1, 28, 0, 1),
        (28, 1, 0, 1, 29, 0, 1), (14, 1, 1, 0, 9, 0, 0), (24, 1, 1, 0, 10, 0, 0), (31, 1, 1, 0, 11, 0, 0),
    ),
    (
        (12, 0, 0, 1, 4, 0, 1), (16, 0, 0, -1, 22, 0, 1), (13, 0, 0, 1, 12, 0, 1), (21, 0, 0, -1, 27, 0, 1),
        (29, 0, 0, 1, 14, 0, 1), (5, 0, 0, -1, 12, 0, 1), None, None,
        (4, 1, 0, 0, 0, 0, 0), (23, 0, 0, 1, 17, 0, 1), (8, 0, 1, -1, 15, 0, 1), (6, 1, 0, 0, 1, 0, 0),
        (22, 0, 0, 1, 19, 0, 1), (9, 0, 1, -1, 18, 0, 1), (7, 1, 0, 0, 2, 0, 0), (30, 0, 0, 1, 22, 0, 1),
        (10, 0, 1, -1, 21, 0, 1), (15, 0, 0, 1, 25, 0, 1), (11, 0, 1, -1, 24, 0, 1), (17, 1, 1, 0, 3, 0, 0),
        (19, 0, 0, 1, 26, 0, 1), (14, 0, 0, -1, 29, 0, 1), (18, 1, 1, 0, 4, 0, 0), (26, 1, 0, 1, 24, 0, 1),
        (24, 0, 1, -1, 30, 0, 1), (20, 1, 1, 0, 5, 0, 0), (25, 1, 0, 1, 27, 0, 1), (31, 0, 0, -1, 31, 0, 1),
        (27, 1, 1, 0, 6, 0, 0), (28, 1, 1, 0, 7, 0, 0), None, None,
    ),
    (
        (14, 0, 0, 1, 3, 0, 1), (8, 0, 0, -1, 10, 0, 1), (31, 0, 0, 1, 6, 0, 1), (9, 0, 0, -1, 13, 0, 1),
        (12, 1, 0, 1, 8, 0, 1), (10, 0, 0, -1, 16, 0, 1), None, (21, 0, 0, 1, 11, 0, 1),
        (11, 0, 0, -1, 18, 0, 1), (16, 0, 0, 1, 13, 0, 1), (24, 0, 0, -1, 24, 0, 1), None,
        (13, 1, 0, 1, 16, 0, 1), (17, 0, 1, -1, 19, 0, 1), (29, 1, 0, 1, 18, 0, 1), (18, 0, 1, -1, 22, 0, 1),
        None, (23, 1, 0, 1, 21, 0, 1), (20, 0, 1, -1, 25, 0, 1), (22, 1, 0, 1, 25, 0, 1),
        (27, 0, 1, -1, 28, 0, 1), None, (30, 1, 0, 1, 27, 0, 1), (28, 0, 1, -1, 29, 0, 1),
        (26, 1, 1, 0, 0, 0, 0), (15, 1, 1, 0, 1, 0, 0), (19, 1, 1, 0, 2, 0, 0), (25, 1, 1, 0, 3, 0, 0),
        None, None, None, None,
    ),
    (
        (24, 0, 0, 1, 3, 0, 1), (25, 0, 0, -1, 27, 0, 1), None, (14, 1, 0, 1, 8, 0, 1),
        (17, 0, 1, -1, 13, 0, 1), None, (31, 1, 0, 1, 10, 0, 1), (18, 0, 1, -1, 15, 0, 1),
        (12, 1, 0, 1, 13, 0, 1), (20, 0, 1, -1, 18, 0, 1), None, (21, 1, 0, 1, 16, 0, 1),
        (28, 0, 1, -1, 23, 0, 1), (16, 1, 0, 1, 17, 0, 1), (27, 0, 1, -1, 20, 0, 1), None,
        (13, 1, 0, 1, 21, 0, 1), (26, 0, 1, -1, 24, 0, 1), (29, 1, 0, 1, 22, 0, 1), (15, 0, 1, -1, 25, 0, 1),
        None, (23, 1, 0, 1, 25, 0, 1), (19, 0, 1, -1, 26, 0, 1), None,
        None, (22, 1, 1, 0, 0, 0, 0), None, (30, 1, 1, 0, 1, 0, 0),
        None, None, None, None,
    ),
    (
        (25, 0, 0, 1, 3, 0, 1), (17, 0, 0, -1, 4, 0, 1), (18, 0, 0, -1, 7, 0, 1), (24, 1, 0, 1, 8, 0, 1),
        (20, 0, 1, -1, 9, 0, 1), None, None, (28, 0, 1, -1, 12, 0, 1),
        (14, 1, 0, 1, 11, 0, 1), (27, 0, 1, -1, 14, 0, 1), (31, 1, 0, 1, 15, 0, 1), None,
        (26, 0, 1, -1, 17, 0, 1), (12, 1, 0, 1, 16, 0, 1), None, (15, 0, 1, -1, 19, 0, 1),
        (21, 1, 0, 1, 19, 0, 1), (16, 1, 0, 1, 21, 0, 1), (19, 0, 1, -1, 22, 0, 1), None,
        (22, 0, 1, -1, 25, 0, 1), (13, 1, 0, 1, 24, 0, 1), (29, 1, 0, 1, 26, 0, 1), (30, 0, 1, -1, 27, 0, 1),
        None, (23, 1, 1, 0, 0, 0, 0), None, None,
        None, None, None, None,
    ),
    (
        (20, 0, 0, -1, 4, 0, 1), None, (28, 0, 0, -1, 7, 0, 1), (25, 1, 0, 1, 8, 0, 1),
        (27, 0, 1, -1, 9, 0, 1), None, None, (26, 0, 1, -1, 12, 0, 1),
        (24, 1, 0, 1, 11, 0, 1), None, None, (14, 1, 0, 1, 15, 0, 1),
        (15, 0, 1, -1, 15, 0, 1), None, (19, 0, 1, -1, 18, 0, 1), (31, 1, 0, 1, 18, 0, 1),
        (12, 1, 0, 1, 20, 0, 1), (22, 0, 1, -1, 20, 0, 1), None, (21, 1, 0, 1, 23, 0, 1),
        (30, 0, 1, -1, 23, 0, 1), (16, 1, 0, 1, 25, 0, 1), (23, 0, 1, -1, 25, 0, 1), None,
        (13, 1, 1, 0, 0, 0, 0), None, (29, 1, 1, 0, 1, 0, 0), None,
        None, None, None, None,
    ),
    (
        (27, 0, 0, -1, 4, 0, 1), (28, 0, 0, 1, 4, 0, 1), (26, 0, 0, -1, 7, 0, 1), None,
        None, None, None, (15, 0, 1, -1, 12, 0, 1),
        (25, 1, 0, 1, 11, 0, 1), None, (19, 0, 1, -1, 14, 0, 1), (24, 1, 0, 1, 15, 0, 1),
        (22, 0, 1, -1, 17, 0, 1), None, None, (14, 1, 0, 1, 21, 0, 1),
        (30, 0, 1, -1, 20, 0, 1), (23, 0, 1, -1, 22, 0, 1), (31, 1, 0, 1, 24, 0, 1), None,
        (12, 1, 0, 1, 26, 0, 1), (13, 0, 1, -1, 24, 0, 1), (29, 0, 1, -1, 26, 0, 1), (21, 1, 0, 1, 28, 0, 1),
        None, (16, 1, 1, 0, 0, 0, 0), None, None,
        None, None, None, None,
    ),
    (
        None, None, None, (15, 0, 1, -1, 7, 0, 1),
        (28, 1, 0, 1, 28, 0, 1), None, None, (19, 0, 1, -1, 10, 0, 1),
        None, (22, 0, 1, -1, 12, 0, 1), None, (25, 1, 0, 1, 23, 0, 1),
        (30, 0, 1, -1, 16, 0, 1), None, (23, 0, 1, -1, 17, 0, 1), (24, 1, 0, 1, 30, 0, 1),
        None, (13, 0, 1, -1, 21, 0, 1), None, None,
        (29, 0, 1, -1, 22, 0, 1), (14, 1, 0, 1, 29, 0, 1), None, (16, 0, 1, -1, 25, 0, 1),
        (31, 1, 0, 1, 31, 0, 1), None, (12, 1, 1, 0, 0, 0, 0), None,
        (21, 1, 1, 0, 1, 0, 0), None, None, None,
    ),
)
LINK_AT = (0, 2, 4, 7, 10, 13, 15, 18, 20)
GRAM_AT = (
    (11, (0, 0, 0, 0, 0, 0, 0, 0), (2, 0, 0, 0, 0, 0, 0, 0)),
    (16, (2, 0, 0, 0, 0, 0, 0, 0), (3, 1, 0, 0, 0, 0, 0, 0)),
    (21, (3, 1, 0, 0, 0, 0, 0, 0), (3, 2, 0, 0, 0, 0, 0, 0)),
    (26, (3, 2, 0, 0, 0, 0, 0, 0), (4, 3, 1, 0, 0, 0, 0, 0)),
    (29, (4, 3, 1, 0, 0, 0, 0, 0), (4, 3, 2, 1, 0, 1, 0, 1)),
    (31, (4, 3, 2, 1, 0, 1, 0, 1), (5, 4, 2, 1, 0, 1, 0, 1)),
    (32, (5, 4, 2, 1, 0, 1, 0, 1), (6, 4, 2, 1, 1, 1, 1, 1)),
)
IDLE = (0, 0, 0, 0, 0, 0, 0)
PAIRS = ((0, 0), (0, 1), (0, 2), (1, 1), (1, 2), (2, 2))


def pick(me, values):
    values = [int(v) for v in values]
    if len(set(values)) == 1:
        return values[0]
    out = jnp.int32(values[-1])
    for p in range(len(values) - 1):
        out = jnp.where(me == p, jnp.int32(values[p]), out)
    return out


def when(cond):
    if isinstance(cond, (bool, int)):
        return (lambda f: f()) if cond else (lambda f: None)
    return pl.when(cond)


def dot(a, b):
    return jnp.dot(a, b, preferred_element_type=F32)


def split(x):
    high = x.astype(BF16)
    return high, (x - high.astype(F32)).astype(BF16)


def kernel(ring, total_steps, inv, couple, cols, rows, var_out, last_full, spread, picks, squares,
           part, roots, got, link_part, link_full, link_put, link_got, keep_h, keep_l, keep_ht, keep_lt,
           b_put, b_got, a_now, a_put, a_got, mat_h, mat_l, tmp_h, tmp_l, last_got,
           state, send_sem, got_sem, lr_send, lr_recv, lg_send, lg_recv, fr_send, fr_recv,
           fg_send, fg_recv, st_send, st_recv, b_send, b_recv, br_send, a_send, a_recv, ar_send):
    me = lax.axis_index("panel")
    t = lax.axis_index("tm")
    m = t // 2
    core = lax.rem(t, 2)
    chips = total_steps // 2
    blk = couple.shape[2]
    local = inv.shape[2]
    width = 3 * blk
    half = blk // SPLIT
    nlocal = local // blk
    levels = len([d for d in (1, 2, 4, 8, 16) if d < chips])
    right = lax.rem(me + 1, ring)
    left = lax.rem(me + ring - 1, ring)
    mate = t + 1 - 2 * core

    def remote(src, dst, ssem, rsem, **where):
        return pltpu.make_async_remote_copy(src_ref=src, dst_ref=dst, send_sem=ssem, recv_sem=rsem,
                                            device_id=where, device_id_type=MESH)

    def arrived(dst, rsem):
        remote(dst, dst, rsem, rsem, tm=t, panel=me).wait_recv()

    def left_here(src, ssem):
        remote(src, src, ssem, ssem, tm=t, panel=me).wait_send()

    def mod(x):
        return lax.rem(x + 4 * ring, ring)

    barrier = pltpu.get_barrier_semaphore()
    greet = [(True, t, lax.rem(me + d, ring)) for d in range(1, ring)] + [(True, mate, me)]
    greet.append((jnp.logical_and(core == 1, t + 1 < total_steps), t + 1, me))
    greet.append((jnp.logical_and(core == 0, t > 0), t - 1, me))
    for k in range(levels):
        d = 2 ** k
        greet.append((jnp.logical_and(core == 0, m + d < chips), t + 2 * d, me))
        greet.append((jnp.logical_and(core == 0, m >= d), t - 2 * d, me))
    for cond, tt, pp in greet:
        @when(cond)
        def _(tt=tt, pp=pp):
            pl.semaphore_signal(barrier, inc=1, device_id=dict(tm=tt, panel=pp), device_id_type=MESH)

    for b in range(nlocal):
        for c in range(3):
            piece = jnp.zeros((blk, blk), F32)
            for k in range(4):
                off = rows[0, k] - (me * nlocal + b)
                piece = piece + couple[c, k].astype(F32) * (1 - jnp.minimum(off * off, 1)).astype(F32)
            spread[pl.ds(b * blk, blk), pl.ds(c * blk, blk)] = piece.astype(BF16)
    later = jnp.minimum(t + 1, total_steps - 1)
    for c in range(3):
        for n in range(SPLIT):
            picks[pl.ds(c * blk + n * half, half), :] = inv[SPLIT * cols[later, c] + n]
    for c in range(3):
        link_part[pl.ds(c * blk, blk), :] = dot(picks[pl.ds(c * blk, blk), :], spread[...])
    peers = jnp.int32(0)
    for cond, tt, pp in greet:
        peers = peers + (1 if cond is True else cond.astype(jnp.int32))
    pl.semaphore_wait(barrier, peers)

    def reduce_step(s, source, size, put, recv, ssem, rsem):
        for way in range(2):
            if s >= 4 - way:
                continue
            nbr = right if way == 0 else left
            r = mod(me + 4 - s) if way == 0 else mod(me - 3 + s)
            src = source.at[pl.ds(pl.multiple_of(r * size, 8), size), :]
            j = 4 * way + s
            if s > 0:
                arrived(recv.at[j - 1], rsem.at[j - 1])
                put[j] = src[...] + recv[j - 1]
                src = put.at[j]
            remote(src, recv.at[j], ssem.at[j], rsem.at[j], panel=nbr).start()

    def reduce_end(source, size, recv, rsem, dest):
        arrived(recv.at[3], rsem.at[3])
        arrived(recv.at[6], rsem.at[6])
        at = pl.ds(pl.multiple_of(me * size, 8), size)
        dest[at, :] = source[at, :] + recv[3] + recv[6]

    def gather_step(s, dest, size, ssem, rsem):
        for way in range(2):
            if s >= 4 - way:
                continue
            nbr = right if way == 0 else left
            r = mod(me - s) if way == 0 else mod(me + s)
            at = pl.ds(pl.multiple_of(r * size, 8), size)
            j = 4 * way + s
            if s > 0:
                arrived(dest.at[at, :], rsem.at[j - 1])
            remote(dest.at[at, :], dest.at[at, :], ssem.at[j], rsem.at[j], panel=nbr).start()

    def gather_end(dest, size, rsem):
        for way in range(2):
            r = mod(me - 4) if way == 0 else mod(me + 3)
            at = pl.ds(pl.multiple_of(r * size, 8), size)
            arrived(dest.at[at, :], rsem.at[3 + 3 * way])

    def spread_start(source, size, recv, ssem, rsem):
        for d in (4, 3, 5, 2, 6, 1, 7):
            r = lax.rem(me + d, ring)
            src = source.at[pl.ds(pl.multiple_of(r * size, 8), size), :]
            remote(src, recv.at[d - 1], ssem.at[d - 1], rsem.at[d - 1], panel=r).start()

    def spread_end(source, size, recv, rsem, dest):
        at = pl.ds(pl.multiple_of(me * size, 8), size)
        x = source[at, :]
        for d in range(1, ring):
            arrived(recv.at[d - 1], rsem.at[d - 1])
            x = x + recv[d - 1]
        dest[at, :] = x

    def share_start(dest, size, ssem, rsem):
        at = pl.ds(pl.multiple_of(me * size, 8), size)
        for d in range(1, ring):
            remote(dest.at[at, :], dest.at[at, :], ssem.at[d - 1], rsem.at[d - 1], panel=lax.rem(me + d, ring)).start()

    def share_end(dest, size, rsem, done):
        for d in (1, 7, 2, 6, 3, 5, 4):
            r = lax.rem(me + ring - d, ring)
            at = pl.ds(pl.multiple_of(r * size, 8), size)
            arrived(dest.at[at, :], rsem.at[d - 1])
            if done is not None:
                done(d, at)

    def halves(n):
        return [pl.ds(0, n // 2), pl.ds(n // 2, n // 2)]

    def ship(src, dst, ssem, rsem, n, h, **where):
        at = halves(src.shape[1])[h]
        remote(src.at[n, at, :], dst.at[n, at, :], ssem.at[n, h], rsem.at[n, h], **where).start()

    def landed(dst, rsem, n, h):
        arrived(dst.at[n, halves(dst.shape[1])[h], :], rsem.at[n, h])

    def shipped(src, ssem, n):
        for h in range(2):
            left_here(src.at[n, halves(src.shape[1])[h], :], ssem.at[n, h])

    def relay(buf, ssem, rsem, n, then=None):
        for h in range(2):
            landed(buf, rsem, n, h)
            @when(core == 0)
            def _(h=h):
                ship(buf, buf, ssem, rsem, n, h, tm=mate)
            if then is not None:
                then(h)

    def sandwich_half(n, v, early, h):
        if h == 0:
            sandwich(a_got.at[n], v, 0, range(3), 0, blk)
        else:
            sandwich(a_got.at[n], v, 1, range(3, 6), blk, 2 * blk, early)

    def keep(v, x):
        h, l = split(x)
        keep_h[v] = h
        keep_l[v] = l
        xt = x.T
        h, l = split(xt)
        keep_ht[v] = h
        keep_lt[v] = l

    def times_kept(x, v):
        h, l = split(x)
        return dot(h, keep_h[v]) + dot(h, keep_l[v]) + dot(l, keep_h[v])

    def unpack(src, write, blocks=range(6)):
        for n in blocks:
            i, j = PAIRS[n]
            x = src[pl.ds(n * blk, blk), :]
            write(i, j, x)
            if i != j:
                write(j, i, x.T)

    def sandwich(src, v, part, blocks, top, count, early=None):
        def write(i, j, x):
            h, l = split(x)
            mat_h[pl.ds(i * blk, blk), pl.ds(j * blk, blk)] = h
            mat_l[pl.ds(i * blk, blk), pl.ds(j * blk, blk)] = l
        unpack(src, write, blocks)
        at = pl.ds(top, count)
        x = dot(mat_h[at, :], keep_h[v]) + dot(mat_h[at, :], keep_l[v]) + dot(mat_l[at, :], keep_h[v])
        h, l = split(x)
        tmp_h[at, :] = h
        tmp_l[at, :] = l
        if part == 0:
            return
        n = 0
        for i in range(3):
            rows_i = pl.ds(i * blk, blk)
            cols_i = pl.ds(i * blk, width - i * blk)
            x = (dot(keep_ht[v, rows_i, :], tmp_h[:, cols_i]) + dot(keep_ht[v, rows_i, :], tmp_l[:, cols_i])
                 + dot(keep_lt[v, rows_i, :], tmp_h[:, cols_i]))
            for j in range(3 - i):
                at = pl.ds(n * blk, blk)
                a_now[at, :] = a_now[at, :] + x[:, j * blk:(j + 1) * blk]
                n += 1
            if i == 0 and early is not None:
                early()

    def add_squares(first, count):
        def one(n, total):
            x = inv[n].astype(F32)
            return total + jnp.sum((x * x).reshape(half // 8, 8, local), axis=0)
        squares[...] = lax.fori_loop(first, first + count, one, squares[...])

    def basis_step(i):
        acts = [ROUTES[p][i] for p in range(ring)]
        active = pick(me, [a is not None for a in acts])
        acts = [a or IDLE for a in acts]
        steps = got.shape[0] // 2

        @when(active == 1)
        def _():
            row = pick(me, [a[0] for a in acts])
            for side in range(2):
                @when(pick(me, [a[1 + side] for a in acts]) == 1)
                def _(side=side):
                    arrived(got.at[side * steps + i], got_sem.at[side * steps + i])
                    part[row] = part[row] + got[side * steps + i]
            slot = pick(me, [a[4] + (steps if a[3] < 0 else 0) for a in acts])

            @when(pick(me, [a[3] != 0 for a in acts]) == 1)
            def _():
                before = pick(me, [a[5] for a in acts])
                @when(before > 0)
                def _():
                    left_here(part.at[0], send_sem.at[before - 1])
                to = pick(me, [(p + acts[p][3]) % ring for p in range(ring)])
                remote(part.at[row], got.at[slot], send_sem.at[i], got_sem.at[slot], panel=to).start()

            @when(pick(me, [a[3] == 0 for a in acts]) == 1)
            def _():
                roots[pl.ds(pl.multiple_of(slot * half, half), half), :] = part[row]

    def add_gram(n, _):
        x = roots[pl.ds(pl.multiple_of(n * 2 * blk, 2 * blk), 2 * blk), :]
        h, l = split(x)
        th, tl = split(x.T)
        n = 0
        for b in range(3):
            at = slice(b * blk, (b + 1) * blk)
            y = dot(th[at], h[:, b * blk:]) + dot(th[at], l[:, b * blk:]) + dot(tl[at], h[:, b * blk:])
            for j in range(3 - b):
                at = pl.ds(n * blk, blk)
                a_now[at, :] = a_now[at, :] + y[:, j * blk:(j + 1) * blk]
                n += 1
        return 0

    def b_first():
        @when(core == 1)
        def _():
            b_put[0] = link_full[...]
            for h in range(2):
                ship(b_put, b_got, b_send, b_recv, 0, h, tm=mate)
        keep(0, link_full[...])

    def b_pair():
        @when(core == 0)
        def _():
            for h in range(2):
                landed(b_got, b_recv, 0, h)
            x = times_kept(b_got[0], 0)
            keep(1, x)
            if levels > 1:
                b_put[1] = x
        @when(core == 1)
        def _():
            keep_h[1] = keep_h[0]
            keep_l[1] = keep_l[0]
            keep_ht[1] = keep_ht[0]
            keep_lt[1] = keep_lt[0]

    def b_sends(k):
        d = 2 ** k
        return jnp.logical_and(core == 0, jnp.logical_and(m >= d, m + d < chips))

    def b_start(k):
        @when(b_sends(k))
        def _():
            for h in range(2):
                ship(b_put, b_got, b_send, b_recv, k + 1, h, tm=t - 2 ** (k + 1))

    def b_relays(k):
        return jnp.logical_and(core == 0, m + 2 ** (k + 1) < chips)

    def b_end(k, which):
        @when(jnp.logical_and(core == which, m + 2 ** (k + 1) < chips))
        def _():
            relay(b_got, br_send, b_recv, k + 1)
            x = times_kept(b_got[k + 1], k + 1)
            keep(k + 2, x)
            if which == 0 and k + 2 < levels:
                b_put[k + 2] = x

    def partial_rows(n, _):
        at = pl.ds(n * 4 * SPLIT, 4 * SPLIT)
        x = dot(inv[at].reshape(4 * blk, local), spread[...])
        part[at] = x.reshape(4 * SPLIT, half, width)
        return 0
    size = width // ring
    reduce_step(0, link_part, size, link_put, link_got, lr_send, lr_recv)
    lax.fori_loop(0, inv.shape[0] // (4 * SPLIT), partial_rows, 0)
    a_now[...] = jnp.zeros_like(a_now)
    roots[...] = jnp.zeros_like(roots)
    squares[...] = jnp.zeros_like(squares)
    nsteps = got.shape[0] // 2
    nblocks = inv.shape[0]
    extra = {}

    def add(i, f):
        extra.setdefault(i, []).append(f)

    for s in range(1, 4):
        add(LINK_AT[s], functools.partial(reduce_step, s, link_part, size, link_put, link_got, lr_send, lr_recv))
    add(LINK_AT[4], functools.partial(reduce_end, link_part, size, link_got, lr_recv, link_full))
    for s in range(4):
        add(LINK_AT[4 + s], functools.partial(gather_step, s, link_full, size, lg_send, lg_recv))
    first = LINK_AT[8]
    add(first, functools.partial(gather_end, link_full, size, lg_recv))
    add(first, b_first)
    add(first + 1, b_pair)
    if levels > 1:
        add(first + 1, functools.partial(b_start, 0))
        add(first + 6, functools.partial(b_end, 0, 0))
        add(first + 7, functools.partial(b_end, 0, 1))
    if levels > 2:
        add(first + 6, functools.partial(b_start, 1))
    for i, low, high in GRAM_AT:
        add(i, lambda low=low, high=high: lax.fori_loop(pick(me, low), pick(me, high), add_gram, 0))
    for i in range(max(nsteps, max(extra) + 1)):
        for f in extra.get(i, []):
            f()
        if i < nsteps:
            basis_step(i)

    def a_ship(k, h):
        @when(jnp.logical_and(core == 0, m >= 2 ** k))
        def _():
            at = halves(6 * blk)[h]
            a_put[k + 1, at, :] = a_now[at, :]
            ship(a_put, a_got, a_send, a_recv, k + 1, h, tm=t - 2 ** (k + 1))

    def a_early(k):
        if k < levels:
            a_ship(k, 0)

    @when(core == 1)
    def _():
        a_put[0] = a_now[...]
        for h in range(2):
            ship(a_put, a_got, a_send, a_recv, 0, h, tm=mate)

    @when(core == 0)
    def _():
        for h in range(2):
            landed(a_got, a_recv, 0, h)
            sandwich_half(0, 0, functools.partial(a_early, 0), h)

    for k in range(levels):
        d = 2 ** k
        if k > 0:
            @when(m + d // 2 >= chips)
            def _(k=k):
                a_early(k)
        a_ship(k, 1)

        if 0 < k and k + 1 < levels:
            b_end(k, 0)
            if k + 2 < levels:
                b_start(k + 1)
        add_squares(k * nblocks // levels, nblocks // levels)

        @when(m + d < chips)
        def _(k=k):
            relay(a_got, ar_send, a_recv, k + 1, functools.partial(sandwich_half, k + 1, k + 1, functools.partial(a_early, k + 1)))
        if 0 < k and k + 1 < levels:
            b_end(k, 1)

    size2 = 6 * blk // ring

    def forward(j, at):
        @when(t > 0)
        def _():
            remote(last_full.at[at, :], state.at[at, :], st_send.at[j], st_recv.at[j], tm=t - 1).start()

    spread_start(a_now, size2, last_got, fr_send, fr_recv)
    spread_end(a_now, size2, last_got, fr_recv, last_full)
    share_start(last_full, size2, fg_send, fg_recv)
    forward(0, pl.ds(pl.multiple_of(me * size2, 8), size2))
    share_end(last_full, size2, fg_recv, forward)

    @when(t + 1 < total_steps)
    def _():
        for d in range(ring):
            r = lax.rem(me + ring - d, ring)
            at = pl.ds(pl.multiple_of(r * size2, 8), size2)
            arrived(state.at[at, :], st_recv.at[d])

    @when(t + 1 == total_steps)
    def _():
        state[...] = jnp.zeros_like(state)

    def write_state(i, j, x):
        h, l = split(x)
        mat_h[pl.ds(i * blk, blk), pl.ds(j * blk, blk)] = h
        mat_l[pl.ds(i * blk, blk), pl.ds(j * blk, blk)] = l
    unpack(state, write_state)
    total = jnp.sum(squares[...], axis=0, keepdims=True)
    y = dot(mat_h[...], picks[...]) + dot(mat_l[...], picks[...])
    var_out[...] = total + jnp.sum(picks[...].astype(F32) * y, axis=0, keepdims=True)

    for i in range(nsteps):
        acts = [ROUTES[p][i] or IDLE for p in range(ring)]
        @when(pick(me, [a[6] for a in acts]) == 1)
        def _(i=i):
            left_here(part.at[0], send_sem.at[i])
    for j in range(ring - 1):
        left_here(link_got.at[j], lr_send.at[j])
        left_here(link_got.at[j], lg_send.at[j])
        left_here(last_got.at[j], fr_send.at[j])
        left_here(last_got.at[j], fg_send.at[j])

    @when(t > 0)
    def _():
        for j in range(ring):
            left_here(last_got.at[0], st_send.at[j])

    @when(core == 1)
    def _():
        shipped(b_got, b_send, 0)
        shipped(a_got, a_send, 0)
    for k in range(levels):
        d = 2 ** k
        if k < levels - 1:
            @when(b_sends(k))
            def _(k=k):
                shipped(b_got, b_send, k + 1)
            @when(b_relays(k))
            def _(k=k):
                shipped(b_got, br_send, k + 1)
        @when(jnp.logical_and(core == 0, m >= d))
        def _(k=k):
            shipped(a_got, a_send, k + 1)
        @when(jnp.logical_and(core == 0, m + d < chips))
        def _(k=k):
            shipped(a_got, ar_send, k + 1)


def finish(var, last, var_out, schur_out):
    blk = last.shape[1]
    var_out[...] = var[...]
    for n, (i, j) in enumerate(PAIRS):
        x = last[pl.ds(n * blk, blk), :]
        schur_out[pl.ds(i * blk, blk), pl.ds(j * blk, blk)] = x
        if i != j:
            schur_out[pl.ds(j * blk, blk), pl.ds(i * blk, blk)] = x.T


def per_device(ring, inv_diag, couple, col_blocks, row_blocks):
    nodes, local = inv_diag.shape[1], inv_diag.shape[2]
    blk = couple.shape[3]
    width = couple.shape[1] * blk
    total_steps = col_blocks.shape[0]
    chips = total_steps // 2
    levels = len([d for d in (1, 2, 4, 8, 16) if d < chips])
    nsteps = len(ROUTES[0])
    half = blk // SPLIT
    piece, piece2 = width // ring, 6 * blk // ring
    vm, dma = pltpu.VMEM, pltpu.SemaphoreType.DMA
    packed = (6 * blk, blk)
    scratch = [
        vm((local, width), BF16), vm((width, local), BF16), vm((8, local), F32),
        vm((nodes // half, half, width), F32), vm((2 * blk * max(GRAM_AT[-1][2]), width), F32), vm((2 * nsteps, half, width), F32),
        vm((width, width), F32), vm((width, width), F32), vm((7, piece, width), F32), vm((7, piece, width), F32),
        vm((levels + 1, width, width), BF16), vm((levels + 1, width, width), BF16),
        vm((levels + 1, width, width), BF16), vm((levels + 1, width, width), BF16),
        vm((levels, width, width), F32), vm((levels, width, width), F32),
        vm(packed, F32), vm((levels + 1,) + packed, F32), vm((levels + 1,) + packed, F32),
        vm((width, width), BF16), vm((width, width), BF16), vm((width, width), BF16), vm((width, width), BF16),
        vm((ring - 1, piece2, blk), F32),
        vm(packed, F32),
        dma((nsteps,)), dma((2 * nsteps,)),
        *[dma((ring - 1,)) for _ in range(8)],
        dma((ring,)), dma((ring,)),
        dma((levels, 2)), dma((levels, 2)), dma((levels, 2)),
        dma((levels + 1, 2)), dma((levels + 1, 2)), dma((levels + 1, 2)),
    ]
    vmem = pl.BlockSpec(memory_space=pltpu.VMEM)
    smem = pl.BlockSpec(memory_space=pltpu.SMEM)
    variances, last = pl.pallas_call(
        functools.partial(kernel, ring, total_steps),
        out_shape=(jax.ShapeDtypeStruct((1, local), F32), jax.ShapeDtypeStruct(packed, F32)),
        in_specs=[vmem, vmem, smem, smem],
        out_specs=(vmem, vmem),
        scratch_shapes=scratch,
        compiler_params=pltpu.CompilerParams(
            collective_id=0, has_side_effects=True, vmem_limit_bytes=56 * 1024 * 1024
        ),
        name="sweep",
    )(inv_diag[0].reshape(nodes // half, half, local), couple[0], col_blocks, row_blocks)
    variances, schur = pl.pallas_call(
        finish,
        out_shape=(jax.ShapeDtypeStruct((1, local), F32), jax.ShapeDtypeStruct((width, width), F32)),
        in_specs=[vmem, vmem],
        out_specs=(vmem, vmem),
        name="finish",
    )(variances, last)
    return variances, schur[None]


def solution(mesh):
    return jax.shard_map(
        functools.partial(per_device, mesh.shape["panel"]),
        mesh=mesh,
        in_specs=(P("tm", None, "panel"), P("tm", None, None, None, None), P(), P("tm", None)),
        out_specs=(P("tm", "panel"), P("tm", None, None)),
        check_vma=False,
    )
```
